32 devices in a mesh: sy: 4 (over z), sx: 8 (over y, x, core).
Axes of the slice: x: 2, y: 2, z: 4, core: 2. Of those that a mesh axis runs over, the one named last changes fastest.
Arguments:
- exposures: bfloat16 [4, 8, 256, 4096], P(None, None, 'sy', 'sx'), may hold values from -6 to 6
- psf_kernels: bfloat16 [4, 8, 21, 21], replicated, may hold values from -0.25 to 0.25
- clip_masks: int32 [4, 8, 256, 4096], P(None, None, 'sy', 'sx'), may hold values from 0 to 255
- exposure_weights: float32 [4, 8], replicated, may hold values from 0.5 to 2
- plane_offsets: int32 [3, 8, 2], replicated, may hold values from -384 to 384, as said below
- start_flux: float32 [8, 256, 4096], P(None, 'sy', 'sx'), may hold values from -6 to 6
- start_weight: float32 [8, 256, 4096], P(None, 'sy', 'sx'), may hold values from 1 to 4
Outputs:
- stacked_flux: float32 [8, 256, 4096], P(None, 'sy', 'sx')
- stacked_weight: float32 [8, 256, 4096], P(None, 'sy', 'sx')
The draws below stay inside these ranges and needn't reach their ends.
Inputs may be any that keep to these rules, and one draw needn't show every extreme that they name: `clip_masks`: bit p of an entry is 1 where plane p clips that pixel of that exposure. plane_offsets[n, p, 0] moves rows and plane_offsets[n, p, 1] moves columns; a row offset has magnitude 64 // 4 to 48, positive for p < 4 and negative otherwise; a column offset has magnitude 512 // 4 to 384, positive for even p and negative for odd p; in every draw some row offset of each sign has magnitude 3 * 16 and some column offset of each sign has magnitude 3 * 128.
All inputs are finite; a program needn't handle non-finite values.
Results may differ from the reference program's by a relative error of at most 0.0003.
Values may be sent and summed in bfloat16 or wider, within the bound.
No kernel may reach another device: no remote copies, remote signals or barrier semaphores. Data moves between devices by JAX's collectives and lax.ppermute only.
A program may use at most 128 MiB of HBM per device.

```python
import math
import jax
import jax.numpy as jnp
from jax import lax

TY = 64
TX = 512
PLANES = 8
NIGHTS = 4
EXPS = 8
KS = 21
NY = 256
NX = 4096


def draw_plane_offsets(key, part):
    folded = jax.random.fold_in(key, 7)
    key_rows, key_cols, key_night, key_plane = jax.random.split(folded, 4)
    table_shape = (NIGHTS - 1, PLANES)
    row_sizes = jax.random.randint(key_rows, table_shape, TY // 4, 3 * TY // 4 + 1)
    col_sizes = jax.random.randint(key_cols, table_shape, TX // 4, 3 * TX // 4 + 1)
    night_pick = jax.random.randint(key_night, (), 0, NIGHTS - 1)
    plane_pick = jax.random.randint(key_plane, (), 0, PLANES // 2)
    night_ids = lax.broadcasted_iota(jnp.int32, table_shape, 0)
    plane_ids = lax.broadcasted_iota(jnp.int32, table_shape, 1)
    on_night = night_ids == night_pick
    row_peak = on_night & ((plane_ids == plane_pick) | (plane_ids == plane_pick + PLANES // 2))
    col_peak = on_night & (plane_ids // 2 == plane_pick)
    row_sizes = jnp.where(row_peak, 3 * TY // 4, row_sizes)
    col_sizes = jnp.where(col_peak, 3 * TX // 4, col_sizes)
    row_signs = jnp.where(plane_ids < PLANES // 2, 1, -1)
    col_signs = 1 - 2 * (plane_ids % 2)
    return jnp.stack([row_sizes * row_signs, col_sizes * col_signs], axis=-1).astype(jnp.int32)


def plant(entries, own_key, least, high):
    index_at = [jax.random.randint(jax.random.fold_in(own_key, axis), (), 0, length) for axis, length in enumerate(entries.shape)]
    main_axis = entries.shape.index(max(entries.shape))
    beside = index_at[:main_axis] + [(index_at[main_axis] + 1) % entries.shape[main_axis]] + index_at[main_axis + 1:]
    return entries.at[tuple(index_at)].set(least).at[tuple(beside)].set(high)


def level_of(key, dims, shards, smallest, top_value):
    def one(position, shards_of):
        heights = jax.random.uniform(jax.random.fold_in(jax.random.fold_in(key, 6), position), (shards_of,), jnp.float32, smallest / len(shards), top_value / len(shards))
        return jnp.repeat(jnp.exp(heights), dims[position] // shards_of).reshape((-1,) + (1,) * (len(dims) - position - 1))

    gain = one(*shards[0])
    for cut in shards[1:]:
        gain = gain * one(*cut)
    return gain


def scatter_about(rng, extent, spread, limit, pieces=(), held_as=jnp.bfloat16):
    loudness = level_of(rng, extent, pieces, -0.22, 0.18) if pieces else 1.0
    values = jax.random.normal(rng, extent, jnp.float32) * spread * loudness
    return jnp.minimum(jnp.maximum(values, -limit), limit).astype(held_as)


def setup_inputs(seed: int = 0) -> dict:
    seeds = jax.random.split(jax.random.key(seed), 8)
    exposures = scatter_about(seeds[0], (NIGHTS, EXPS, NY, NX), 1.0, 6.0, ((2, 4), (3, 8)))
    psf_kernels = scatter_about(seeds[1], (NIGHTS, EXPS, KS, KS), (KS * KS) ** -0.5, 0.25)
    clip_masks = plant(jax.random.randint(seeds[2], (NIGHTS, EXPS, NY, NX), 0, 2 ** PLANES), jax.random.fold_in(seeds[2], 1), 0, (2 ** PLANES) - 1).astype(jnp.int32)
    exposure_weights = jnp.clip(jnp.exp(jax.random.uniform(seeds[3], (NIGHTS, EXPS), jnp.float32, math.log(0.5), math.log(2.0))), 0.5, 2.0)
    plane_offsets = draw_plane_offsets(jax.random.fold_in(seeds[7], 71), 0)
    start_flux = scatter_about(seeds[5], (PLANES, NY, NX), 1.0, 6.0, ((1, 4), (2, 8)), jnp.float32)
    start_weight = jnp.clip(jnp.exp(math.log(4.0) - 1.3862944 * jax.random.uniform(seeds[6], (PLANES, NY, NX), jnp.float32) ** level_of(seeds[6], (PLANES, NY, NX), ((1, 4), (2, 8)), -0.2, 0.2)), 1.0, 4.0)
    return {"exposures": exposures, "psf_kernels": psf_kernels, "clip_masks": clip_masks, "exposure_weights": exposure_weights, "plane_offsets": plane_offsets, "start_flux": start_flux, "start_weight": start_weight}


band_scale = 1.5
weight_floor = 1.0

def psf_filter(image, kernel):
    image_wide = image.astype(jnp.float32)
    kernel_wide = kernel.astype(jnp.float32)
    kernel_size = kernel.shape[0]
    radius = (kernel_size - 1) // 2
    rows_full = image.shape[0] + 2 * radius
    cols_full = image.shape[1] + 2 * radius
    padded = jnp.pad(image_wide, radius)
    kernel_padded = jnp.pad(kernel_wide, ((0, rows_full - kernel_size), (0, cols_full - kernel_size)))
    product = jnp.fft.rfft2(padded) * jnp.conj(jnp.fft.rfft2(kernel_padded))
    result = jnp.fft.irfft2(product, s=(rows_full, cols_full))
    return result[:image.shape[0], :image.shape[1]]

def shift_field(field, row_offset, column_offset):
    margin_rows = 3 * TY // 4
    margin_cols = 3 * TX // 4
    padded = jnp.pad(field, ((margin_rows, margin_rows), (margin_cols, margin_cols)))
    first_row = (margin_rows - row_offset).astype(jnp.int32)
    first_col = (margin_cols - column_offset).astype(jnp.int32)
    return lax.dynamic_slice(padded, (first_row, first_col), (NY, NX))

def plane_update(flux_plane, weight_plane, power, filtered, clip_mask, weight_value):
    clip_bits = clip_mask // power % 2
    running_mean = flux_plane / jnp.maximum(weight_plane, weight_floor)
    band_half = band_scale / jnp.sqrt(weight_value)
    clipped = jnp.clip(filtered, running_mean - band_half, running_mean + band_half)
    chosen = jnp.where(clip_bits == 1, clipped, filtered)
    return (flux_plane + weight_value * chosen, weight_plane + weight_value)

def move_plane(plane_items):
    flux_plane, weight_plane, row_offset, column_offset = plane_items
    return (shift_field(flux_plane, row_offset, column_offset), shift_field(weight_plane, row_offset, column_offset))

def reference(exposures, psf_kernels, clip_masks, exposure_weights, plane_offsets, start_flux, start_weight):
    powers = 2 ** jnp.arange(PLANES, dtype=jnp.int32)
    flux_stack = start_flux
    weight_stack = start_weight
    for night_index in range(NIGHTS):
        if night_index > 0:
            offsets_now = plane_offsets[night_index - 1]
            flux_stack, weight_stack = lax.map(move_plane, (flux_stack, weight_stack, offsets_now[:, 0], offsets_now[:, 1]))

        def exposure_step(frame_index, carried):
            filtered = psf_filter(exposures[night_index, frame_index], psf_kernels[night_index, frame_index])
            weight_value = exposure_weights[night_index, frame_index]
            clip_mask = clip_masks[night_index, frame_index]

            def update_one(plane_items):
                return plane_update(plane_items[0], plane_items[1], plane_items[2], filtered, clip_mask, weight_value)
            return lax.map(update_one, (carried[0], carried[1], powers))
        flux_stack, weight_stack = lax.fori_loop(0, EXPS, exposure_step, (flux_stack, weight_stack))
    return (flux_stack, weight_stack)
```

```python
import functools

import jax
import jax.numpy as jnp
from jax import lax
from jax.experimental import pallas as pl
from jax.experimental.pallas import tpu as pltpu
from jax.sharding import PartitionSpec as P

band_scale = 1.5
weight_floor = 1.0
LANES = 128
SUB = 8
GROUP = 16
bf16 = jnp.bfloat16
f32 = jnp.float32
VMEM_LIMIT = 48 * 1024 * 1024


def swap_pairs(axis, parity):
    ny, nx = lax.axis_size("sy"), lax.axis_size("sx")
    count, others = (ny, nx) if axis == "sy" else (nx, ny)
    pairs = []
    for j in range(others):
        for i in range(count):
            k = i + 1 if (i - parity) % 2 == 0 else i - 1
            target = (k, j) if 0 <= k < count else (i, j ^ 1)
            if axis == "sy":
                pairs.append((i * nx + j, target[0] * nx + target[1]))
            else:
                pairs.append((j * nx + i, target[1] * nx + target[0]))
    return pairs


def swap(value, axis, parity):
    return lax.ppermute(value, ("sy", "sx"), swap_pairs(axis, parity))


def encode(v):
    v2 = v * v
    v4 = v2 * v2
    return (v4 * v2 * v).astype(bf16)


def decode(code):
    y = code.astype(f32)
    size = jnp.exp2(jnp.log2(jnp.abs(y)) * (1.0 / 7.0))
    size = jnp.where(y == 0.0, 0.0, size)
    return jnp.where(y < 0.0, -size, size)


def lane_iota(shape):
    return lax.broadcasted_iota(jnp.int32, shape, len(shape) - 1)


def pack_rows_kernel(info, x_top, x_bot, send_a, send_b, *, radius):
    nights, frames = x_top.shape[0], x_top.shape[1]
    rows = frames * radius
    even = info[0] == 0
    shape = (rows, frames * GROUP)
    r = lax.broadcasted_iota(jnp.int32, shape, 0)
    c = lax.broadcasted_iota(jnp.int32, shape, 1)
    base = (r // radius) * GROUP + r % radius
    sel_top = (c == base).astype(bf16)
    sel_bot = (c == base + (GROUP - radius)).astype(bf16)
    for n in range(nights):
        up = x_top[n].reshape(frames * GROUP, x_top.shape[3])
        down = x_bot[n].reshape(frames * GROUP, x_bot.shape[3])
        up = jnp.dot(sel_top, up, preferred_element_type=f32).astype(bf16)
        down = jnp.dot(sel_bot, down, preferred_element_type=f32).astype(bf16)
        send_a[n] = jnp.where(even, down, up)
        send_b[n] = jnp.where(even, up, down)


def pack_rows(info, exposures, first, count, radius):
    nights, frames, rows, cols = exposures.shape
    out = jax.ShapeDtypeStruct((count, frames * radius, cols), bf16)
    x = exposures[first : first + count]
    last = rows // GROUP - 1
    return pl.pallas_call(
        functools.partial(pack_rows_kernel, radius=radius),
        grid=(1,),
        out_shape=(out, out),
        in_specs=[
            pl.BlockSpec(memory_space=pltpu.SMEM),
            pl.BlockSpec((count, frames, GROUP, cols), lambda i: (0, 0, 0, 0)),
            pl.BlockSpec((count, frames, GROUP, cols), lambda i: (0, 0, last, 0)),
        ],
        out_specs=(pl.BlockSpec(out.shape, lambda i: (0, 0, 0)),) * 2,
        compiler_params=pltpu.CompilerParams(vmem_limit_bytes=VMEM_LIMIT),
        name="pack_rows",
    )(info, x, x)


def pack_cols_kernel(info, x_left, x_right, la, lb, ra, rb, send_a, send_b, *, radius):
    nights, frames, rows = x_left.shape[0], x_left.shape[1], x_left.shape[2]
    even_y = info[0] == 0
    even_x = info[1] == 0
    lane = lane_iota((rows, LANES))
    halo_lane = lane_iota((frames * radius, LANES))
    for n in range(nights):
        to_right = jnp.zeros((rows, LANES), bf16)
        to_left = jnp.zeros((rows, LANES), bf16)
        for e in range(frames):
            here = (lane >= radius * e) & (lane < radius * (e + 1))
            shift = (radius * (e + 1)) % LANES
            to_right = jnp.where(here, pltpu.roll(x_right[n, e], shift, 1), to_right)
            to_left = jnp.where(here, pltpu.roll(x_left[n, e], radius * e, 1), to_left)
        top_l = jnp.where(even_y, lb[n], la[n])
        bot_l = jnp.where(even_y, la[n], lb[n])
        top_r = jnp.where(even_y, rb[n], ra[n])
        bot_r = jnp.where(even_y, ra[n], rb[n])
        corner_right = jnp.where(
            halo_lane < radius, pltpu.roll(top_r, radius, 1), pltpu.roll(bot_r, 2 * radius, 1)
        )
        corner_left = jnp.where(halo_lane < radius, top_l, pltpu.roll(bot_l, radius, 1))
        send_a[n, :rows] = jnp.where(even_x, to_right, to_left)
        send_b[n, :rows] = jnp.where(even_x, to_left, to_right)
        send_a[n, rows:] = jnp.where(even_x, corner_right, corner_left)
        send_b[n, rows:] = jnp.where(even_x, corner_left, corner_right)


def pack_cols(info, exposures, recv_a, recv_b, first, count, radius):
    nights, frames, rows, cols = exposures.shape
    out = jax.ShapeDtypeStruct((count, rows + frames * radius, LANES), bf16)
    x = exposures[first : first + count]
    last = cols // LANES - 1
    halo = (count, frames * radius, LANES)
    return pl.pallas_call(
        functools.partial(pack_cols_kernel, radius=radius),
        grid=(1,),
        out_shape=(out, out),
        in_specs=[
            pl.BlockSpec(memory_space=pltpu.SMEM),
            pl.BlockSpec((count, frames, rows, LANES), lambda i: (0, 0, 0, 0)),
            pl.BlockSpec((count, frames, rows, LANES), lambda i: (0, 0, 0, last)),
            pl.BlockSpec(halo, lambda i: (0, 0, 0)),
            pl.BlockSpec(halo, lambda i: (0, 0, 0)),
            pl.BlockSpec(halo, lambda i: (0, 0, last)),
            pl.BlockSpec(halo, lambda i: (0, 0, last)),
        ],
        out_specs=(pl.BlockSpec(out.shape, lambda i: (0, 0, 0)),) * 2,
        compiler_params=pltpu.CompilerParams(vmem_limit_bytes=VMEM_LIMIT),
        name="pack_cols",
    )(info, x, x, recv_a, recv_b, recv_a, recv_b)


def filter_kernel(
    info, x, ra, rb, ca, cb, taps, out, border, image, windows, *, radius, pitch
):
    frames, rows, cols = x.shape[1], x.shape[2], x.shape[3]
    tiles = cols // LANES
    size = 2 * radius + 1
    packed = frames * radius
    extra = pitch - rows
    even_y = info[0] == 0
    even_x = info[1] == 0
    zero = jnp.zeros((), bf16)
    top_ok = info[2] > 0
    bot_ok = info[2] < info[4] - 1
    left_ok = info[3] > 0
    right_ok = info[3] < info[5] - 1

    col_l = jnp.where(left_ok, jnp.where(even_x, cb[0], ca[0]), zero)
    col_r = jnp.where(right_ok, jnp.where(even_x, ca[0], cb[0]), zero)
    halo_lane = lane_iota((packed, LANES))
    corner_l, corner_r = col_l[rows:], col_r[rows:]
    side_top = jnp.where(
        halo_lane < radius,
        corner_r,
        jnp.where(halo_lane >= LANES - radius, pltpu.roll(corner_l, LANES - radius, 1), zero),
    )
    side_bot = jnp.where(
        halo_lane < radius,
        pltpu.roll(corner_r, LANES - radius, 1),
        jnp.where(halo_lane >= LANES - radius, pltpu.roll(corner_l, LANES - 2 * radius, 1), zero),
    )
    top = jnp.concatenate([jnp.where(even_y, rb[0], ra[0]), side_top], axis=1)
    bot = jnp.concatenate([jnp.where(even_y, ra[0], rb[0]), side_bot], axis=1)
    top = jnp.where(top_ok, top, zero)
    bot = jnp.where(bot_ok, bot, zero)
    top = pltpu.roll(top, cols + LANES - 1, 1)
    shape = (frames * extra, packed)
    r = lax.broadcasted_iota(jnp.int32, shape, 0)
    c = lax.broadcasted_iota(jnp.int32, shape, 1)
    frame, place = r // extra, r % extra
    sel_bot = ((place < radius) & (c == frame * radius + place)).astype(bf16)
    from_top = place - (extra - radius)
    sel_top = ((from_top >= 0) & (c == frame * radius + from_top)).astype(bf16)
    border[...] = (
        jnp.dot(sel_bot, bot, preferred_element_type=f32)
        + jnp.dot(sel_top, top, preferred_element_type=f32)
    ).astype(bf16)

    lane = lane_iota((rows, LANES))
    lane_all = lane_iota((pitch, LANES))
    depth = windows.shape[0]

    def one(e, carry):
        image[:rows, :cols] = x[0, e]
        side_r = pltpu.roll(col_r[:rows], (LANES - radius * e) % LANES, 1)
        side_l = pltpu.roll(col_l[:rows], (2 * LANES - radius - radius * e) % LANES, 1)
        image[:rows, cols:] = jnp.where(
            lane < radius, side_r, jnp.where(lane >= LANES - radius, side_l, zero)
        )
        image[rows:] = border[pl.ds(pl.multiple_of(e * extra, extra), extra)]
        parts = [image[:, LANES * k : LANES * (k + 1)] for k in range(tiles + 1)]

        def window(shift, source, mask_lane):
            turned = [pltpu.roll(t, shift % LANES, 1) if shift else t for t in source]
            result = []
            for k in range(tiles):
                if shift > 0:
                    result.append(jnp.where(mask_lane < shift, turned[k - 1], turned[k]))
                elif shift < 0:
                    result.append(jnp.where(mask_lane < LANES + shift, turned[k], turned[k + 1]))
                else:
                    result.append(turned[k])
            return result

        for b in range(size):
            for k, value in enumerate(window(radius - b, parts, lane_all)):
                windows[pitch * b : pitch * (b + 1), LANES * k : LANES * (k + 1)] = value
        tail = [t[rows:] for t in parts]
        for k, value in enumerate(window(radius + 1, tail, lane_all[:extra])):
            windows[pitch * size : pitch * size + extra, LANES * k : LANES * (k + 1)] = value
        row = jnp.broadcast_to(taps[0, pl.ds(e, 1), :], (rows, depth))
        band = pltpu.roll(row, 0, 1, stride=1, stride_axis=0).astype(bf16)
        out[e] = jnp.dot(band, windows[...], preferred_element_type=f32)
        return carry

    lax.fori_loop(0, frames, one, 0)


def filter_night(info, exposures, night, half, taps, rows_a, rows_b, cols_a, cols_b, radius):
    nights, frames, rows, cols = exposures.shape
    pitch = rows + 2 * GROUP
    depth = taps.shape[2]
    packed = frames * radius
    return pl.pallas_call(
        functools.partial(filter_kernel, radius=radius, pitch=pitch),
        grid=(1,),
        out_shape=jax.ShapeDtypeStruct((frames, rows, cols), f32),
        in_specs=[
            pl.BlockSpec(memory_space=pltpu.SMEM),
            pl.BlockSpec((1, frames, rows, cols), lambda i: (night, 0, 0, 0)),
            pl.BlockSpec((1, packed, cols), lambda i: (half, 0, 0)),
            pl.BlockSpec((1, packed, cols), lambda i: (half, 0, 0)),
            pl.BlockSpec((1, rows + packed, LANES), lambda i: (half, 0, 0)),
            pl.BlockSpec((1, rows + packed, LANES), lambda i: (half, 0, 0)),
            pl.BlockSpec((1, frames, depth), lambda i: (night, 0, 0)),
        ],
        out_specs=pl.BlockSpec((frames, rows, cols), lambda i: (0, 0, 0)),
        scratch_shapes=[
            pltpu.VMEM((frames * 2 * GROUP, cols + LANES), bf16),
            pltpu.VMEM((pitch, cols + LANES), bf16),
            pltpu.VMEM((depth, cols), bf16),
        ],
        compiler_params=pltpu.CompilerParams(vmem_limit_bytes=VMEM_LIMIT),
        cost_estimate=pl.CostEstimate(
            flops=2 * frames * rows * depth * cols, bytes_accessed=4 << 20, transcendentals=0
        ),
        name="filter_night",
    )(info, exposures, rows_a, rows_b, cols_a, cols_b, taps)


def tap_rows(psf_kernels, tile_rows):
    nights, frames, size, _ = psf_kernels.shape
    radius = (size - 1) // 2
    pitch = tile_rows + 2 * GROUP
    by_column = jnp.swapaxes(psf_kernels, 2, 3).astype(f32)
    wide = jnp.pad(by_column, ((0, 0), (0, 0), (0, 0), (0, pitch - size)))
    flat = wide.reshape(nights, frames, size * pitch)
    flat = jnp.pad(flat, ((0, 0), (0, 0), (0, 2 * GROUP)))
    return jnp.concatenate([flat[:, :, radius:], flat[:, :, :radius]], axis=2)


def row_strips(info, load, planes, margin, tile_rows, send_a, send_b):
    half = planes // 2
    odd = info[0]

    def one(k, carry):
        low = pl.multiple_of((tile_rows - margin) * (1 - odd), SUB)
        high = pl.multiple_of((tile_rows - margin) * odd, SUB)
        send_a[k] = encode(load(k + half * odd, pl.ds(low, margin)))
        send_b[k] = encode(load(k + half * (1 - odd), pl.ds(high, margin)))
        return carry

    lax.fori_loop(0, half, one, 0)


def first_strips_kernel(info, sums, field, send_a, send_b, *, margin):
    planes, rows, cols = field.shape
    row_strips(
        info, lambda p, r: field[p, r, :] + sums[0], planes, margin, rows, send_a, send_b
    )


def first_strips(info, sums, field):
    planes, rows, cols = field.shape
    margin = 3 * rows // 4
    out = jax.ShapeDtypeStruct((planes // 2, margin, cols), bf16)
    return pl.pallas_call(
        functools.partial(first_strips_kernel, margin=margin),
        out_shape=(out, out),
        in_specs=[
            pl.BlockSpec(memory_space=pltpu.SMEM),
            pl.BlockSpec(memory_space=pltpu.SMEM),
            pl.BlockSpec(memory_space=pltpu.VMEM),
        ],
        out_specs=(pl.BlockSpec(memory_space=pltpu.VMEM),) * 2,
        compiler_params=pltpu.CompilerParams(vmem_limit_bytes=VMEM_LIMIT),
        name="first_strips",
    )(info, sums, field)


def move_rows_kernel(
    info, offsets, sums, field, ra, rb, out, send_a, send_b, above, *, margin, side
):
    planes, rows, cols = field.shape
    half = planes // 2
    odd = info[0]
    odd_x = info[1]
    top_ok = jnp.where(info[2] > 0, 1.0, 0.0)
    bot_ok = jnp.where(info[2] < info[4] - 1, 1.0, 0.0)
    sub = lax.broadcasted_iota(jnp.int32, (SUB, cols), 0)
    add = sums[0]

    def turn(start):
        base = pl.multiple_of((start // SUB) * SUB, SUB)
        rest = start % SUB
        back = (SUB - rest) % SUB
        keep = sub < SUB - rest
        turned = [
            pltpu.roll(above[pl.ds(pl.multiple_of(base + SUB * j, SUB), SUB), :], back, 0)
            for j in range(rows // SUB + 1)
        ]
        return [
            jnp.where(keep, turned[j], turned[j + 1]) for j in range(rows // SUB)
        ]

    def down(k, carry):
        got = jnp.where(odd == 0, rb[k].astype(f32), ra[k].astype(f32))
        above[:margin] = decode(got) * top_ok
        above[margin : margin + rows] = field[k] + add
        for j, value in enumerate(turn(margin - offsets[2 * k])):
            out[k, SUB * j : SUB * (j + 1), :] = value
        return carry

    def up(k, carry):
        p = k + half
        got = jnp.where(odd == 0, ra[k].astype(f32), rb[k].astype(f32))
        above[:rows] = field[p] + add
        above[rows : rows + margin] = decode(got) * bot_ok
        for j, value in enumerate(turn(-offsets[2 * p])):
            out[p, SUB * j : SUB * (j + 1), :] = value
        return carry

    above[rows + margin :] = jnp.zeros((above.shape[0] - rows - margin, cols), f32)
    lax.fori_loop(0, half, down, 0)
    lax.fori_loop(0, half, up, 0)

    def strips(k, carry):
        right = pl.multiple_of((cols - side) * (1 - odd_x), LANES)
        left = pl.multiple_of((cols - side) * odd_x, LANES)
        send_a[k] = encode(out[2 * k + odd_x, :, pl.ds(right, side)])
        send_b[k] = encode(out[2 * k + 1 - odd_x, :, pl.ds(left, side)])
        return carry

    lax.fori_loop(0, half, strips, 0)


def move_rows(info, offsets, sums, field, recv_a, recv_b):
    planes, rows, cols = field.shape
    margin = 3 * rows // 4
    side = 3 * cols // 4
    strip = jax.ShapeDtypeStruct((planes // 2, rows, side), bf16)
    smem = pl.BlockSpec(memory_space=pltpu.SMEM)
    vmem = pl.BlockSpec(memory_space=pltpu.VMEM)
    return pl.pallas_call(
        functools.partial(move_rows_kernel, margin=margin, side=side),
        out_shape=(jax.ShapeDtypeStruct(field.shape, f32), strip, strip),
        in_specs=[smem, smem, smem, vmem, vmem, vmem],
        out_specs=(vmem, vmem, vmem),
        scratch_shapes=[pltpu.VMEM((rows + margin + SUB, cols), f32)],
        compiler_params=pltpu.CompilerParams(vmem_limit_bytes=VMEM_LIMIT),
        name="move_rows",
    )(info, offsets, sums, field, recv_a, recv_b)


def move_columns(info, offsets, field, ca, cb, out, wide, side):
    planes, rows, cols = field.shape
    half = planes // 2
    odd_x = info[1]
    left_ok = jnp.where(info[3] > 0, 1.0, 0.0)
    right_ok = jnp.where(info[3] < info[5] - 1, 1.0, 0.0)
    lane = lane_iota((rows, LANES))
    tiles = cols // LANES

    def turn(start):
        base = (start // LANES) * LANES
        rest = start % LANES
        back = (LANES - rest) % LANES
        keep = lane < LANES - rest
        turned = [
            pltpu.roll(wide[:, pl.ds(pl.multiple_of(base + LANES * j, LANES), LANES)], back, 1)
            for j in range(tiles + 1)
        ]
        return [jnp.where(keep, turned[j], turned[j + 1]) for j in range(tiles)]

    wide[:, cols + side :] = jnp.zeros((rows, wide.shape[1] - cols - side), f32)

    def one(k, carry):
        got = jnp.where(odd_x == 0, cb[k].astype(f32), ca[k].astype(f32))
        wide[:, :side] = decode(got) * left_ok
        wide[:, side : side + cols] = field[2 * k]
        for j, value in enumerate(turn(side - offsets[4 * k + 1])):
            out[2 * k, :, LANES * j : LANES * (j + 1)] = value
        got = jnp.where(odd_x == 0, ca[k].astype(f32), cb[k].astype(f32))
        wide[:, :cols] = field[2 * k + 1]
        wide[:, cols : cols + side] = decode(got) * right_ok
        for j, value in enumerate(turn(-offsets[4 * k + 3])):
            out[2 * k + 1, :, LANES * j : LANES * (j + 1)] = value
        return carry

    lax.fori_loop(0, half, one, 0)


def move_cols_kernel(
    info, offsets, sums, field, ca, cb, out, *rest, margin, side, more
):
    planes, rows, cols = field.shape
    wide = rest[-1]
    move_columns(info, offsets, field, ca, cb, out, wide, side)
    if more:
        row_strips(
            info, lambda p, r: out[p, r, :] + sums[0], planes, margin, rows, rest[0], rest[1]
        )


def move_cols(info, offsets, sums, field, recv_a, recv_b, more):
    planes, rows, cols = field.shape
    margin = 3 * rows // 4
    side = 3 * cols // 4
    strip = jax.ShapeDtypeStruct((planes // 2, margin, cols), bf16)
    smem = pl.BlockSpec(memory_space=pltpu.SMEM)
    vmem = pl.BlockSpec(memory_space=pltpu.VMEM)
    strips = 2 if more else 0
    return pl.pallas_call(
        functools.partial(move_cols_kernel, margin=margin, side=side, more=more),
        out_shape=(jax.ShapeDtypeStruct(field.shape, f32),) + (strip,) * strips,
        in_specs=[smem, smem, smem, vmem, vmem, vmem],
        out_specs=(vmem,) * (1 + strips),
        scratch_shapes=[pltpu.VMEM((rows, cols + side + LANES), f32)],
        compiler_params=pltpu.CompilerParams(vmem_limit_bytes=VMEM_LIMIT),
        name="move_cols",
    )(info, offsets, sums, field, recv_a, recv_b)


def stack_kernel(*refs, moved, last, margin, side):
    info, offsets, weights, flux, weight, filtered, masks = refs[:7]
    if moved:
        ca, cb = refs[7:9]
        outs = refs[9:]
    else:
        outs = refs[7:]
    planes, rows, cols = flux.shape
    frames = filtered.shape[0]
    out = outs[0]
    if moved:
        move_columns(info, offsets, flux, ca, cb, out, outs[-1], side)
        source = out
    else:
        source = flux
    tiles = cols // LANES
    gain = [weights[e] for e in range(frames)]
    band = [
        band_scale / jnp.sqrt(jnp.full((SUB, LANES), gain[e], f32)) for e in range(frames)
    ]

    def chunk(i, carry):
        r = pl.ds(pl.multiple_of((i // tiles) * SUB, SUB), SUB)
        c = pl.ds(pl.multiple_of((i % tiles) * LANES, LANES), LANES)
        value = [filtered[e, r, c] for e in range(frames)]
        mask = [masks[0, e, r, c] for e in range(frames)]
        for p in range(planes):
            f = source[p, r, c]
            w = weight[p, r, c]
            for e in range(frames):
                mean = f * pl.reciprocal(jnp.maximum(w, weight_floor), approx=True)
                clipped = jnp.minimum(jnp.maximum(value[e], mean - band[e]), mean + band[e])
                chosen = jnp.where((mask[e] & (1 << p)) != 0, clipped, value[e])
                f = f + gain[e] * chosen
                w = w + gain[e]
            out[p, r, c] = f
            if last:
                outs[1][p, r, c] = w
        return carry

    lax.fori_loop(0, (rows // SUB) * tiles, chunk, 0)
    if not last:
        row_strips(
            info, lambda p, r: out[p, r, :], planes, margin, rows, outs[1], outs[2]
        )


def stack_night(info, offsets, weights, flux, weight, filtered, masks, night, recv, last):
    planes, rows, cols = flux.shape
    frames = masks.shape[1]
    margin = 3 * rows // 4
    side = 3 * cols // 4
    moved = recv is not None
    smem = pl.BlockSpec(memory_space=pltpu.SMEM)

    def whole(shape):
        return pl.BlockSpec(shape, lambda i: (0,) * len(shape))

    field = jax.ShapeDtypeStruct(flux.shape, f32)
    strip = jax.ShapeDtypeStruct((planes // 2, margin, cols), bf16)
    outs = (field, field) if last else (field, strip, strip)
    return pl.pallas_call(
        functools.partial(stack_kernel, moved=moved, last=last, margin=margin, side=side),
        grid=(1,),
        out_shape=outs,
        in_specs=[
            smem,
            smem,
            smem,
            whole(flux.shape),
            whole(weight.shape),
            whole(filtered.shape),
            pl.BlockSpec((1, frames, rows, cols), lambda i: (night, 0, 0, 0)),
        ]
        + ([whole(recv[0].shape)] * 2 if moved else []),
        out_specs=tuple(whole(o.shape) for o in outs),
        scratch_shapes=[pltpu.VMEM((rows, cols + side + LANES), f32)] if moved else [],
        compiler_params=pltpu.CompilerParams(vmem_limit_bytes=VMEM_LIMIT),
        cost_estimate=pl.CostEstimate(
            flops=12 * frames * planes * rows * cols, bytes_accessed=4 << 20, transcendentals=0
        ),
        name="stack_night",
    )(info, offsets, weights, flux, weight, filtered, masks, *(recv if moved else ()))


def per_device(
    exposures, psf_kernels, clip_masks, exposure_weights, plane_offsets, start_flux, start_weight
):
    nights, frames, rows, cols = exposures.shape
    radius = (psf_kernels.shape[2] - 1) // 2
    iy, ix = lax.axis_index("sy"), lax.axis_index("sx")
    ny, nx = lax.axis_size("sy"), lax.axis_size("sx")
    info = jnp.stack([iy % 2, ix % 2, iy, ix, jnp.int32(ny), jnp.int32(nx)]).astype(jnp.int32)
    offsets = [plane_offsets[n].reshape(-1) for n in range(nights - 1)]
    gains = [exposure_weights[n] for n in range(nights)]
    sums = [jnp.sum(exposure_weights[n]).reshape(1) for n in range(nights)]
    nothing = jnp.zeros((1,), f32)
    taps = tap_rows(psf_kernels, rows)

    halos = []
    for first, count in ((0, 1), (1, nights - 1)):
        sent = pack_rows(info, exposures, first, count, radius)
        got_rows = [swap(s, "sy", i) for i, s in enumerate(sent)]
        sent = pack_cols(info, exposures, *got_rows, first, count, radius)
        got_cols = [swap(s, "sx", i) for i, s in enumerate(sent)]
        halos.append((got_rows, got_cols))

    def filtered(n):
        got_rows, got_cols = halos[min(n, 1)]
        half = 0 if n == 0 else n - 1
        return filter_night(info, exposures, n, half, taps, *got_rows, *got_cols, radius)

    weight = [start_weight]
    strips = first_strips(info, sums[0], start_weight)
    for n in range(1, nights):
        got = [swap(s, "sy", i) for i, s in enumerate(strips)]
        moved, *sides = move_rows(info, offsets[n - 1], sums[n - 1], weight[-1], *got)
        got = [swap(s, "sx", i) for i, s in enumerate(sides)]
        new, *strips = move_cols(info, offsets[n - 1], sums[n], moved, *got, n < nights - 1)
        weight.append(new)

    flux = start_flux
    recv = None
    for n in range(nights):
        last = n == nights - 1
        flux, *more = stack_night(
            info, offsets[max(n - 1, 0)], gains[n], flux, weight[n], filtered(n), clip_masks, n,
            recv, last,
        )
        if last:
            return flux, more[0]
        got = [swap(s, "sy", i) for i, s in enumerate(more)]
        flux, *sides = move_rows(info, offsets[n], nothing, flux, *got)
        recv = [swap(s, "sx", i) for i, s in enumerate(sides)]


def solution(mesh):
    return jax.shard_map(
        per_device,
        mesh=mesh,
        in_specs=(
            P(None, None, "sy", "sx"),
            P(),
            P(None, None, "sy", "sx"),
            P(),
            P(),
            P(None, "sy", "sx"),
            P(None, "sy", "sx"),
        ),
        out_specs=(P(None, "sy", "sx"), P(None, "sy", "sx")),
        check_vma=False,
    )
```

```python
import functools
import math

import jax
import jax.numpy as jnp
from jax import lax
from jax.experimental import pallas as pl
from jax.experimental.pallas import tpu as pltpu
from jax.sharding import PartitionSpec as P

band_scale = 1.5
weight_floor = 1.0
LANES = 128
SUB = 8
GROUP = 16
bf16 = jnp.bfloat16
f32 = jnp.float32
SMEM = pl.BlockSpec(memory_space=pltpu.SMEM)
VMEM = pl.BlockSpec(memory_space=pltpu.VMEM)


def call(kernel, outs, in_specs, args, *, name, flops, scratch=(), limit=16 << 20):
    size = sum(math.prod(o.shape) * o.dtype.itemsize for o in outs)
    return pl.pallas_call(
        kernel,
        out_shape=tuple(outs),
        in_specs=in_specs,
        out_specs=(VMEM,) * len(outs),
        scratch_shapes=list(scratch),
        compiler_params=pltpu.CompilerParams(vmem_limit_bytes=limit),
        cost_estimate=pl.CostEstimate(flops=flops, bytes_accessed=2 * size, transcendentals=0),
        name=name,
    )(*args)


def swap_pairs(axis, parity):
    ny, nx = lax.axis_size("sy"), lax.axis_size("sx")
    count, others = (ny, nx) if axis == "sy" else (nx, ny)
    pairs = []
    for j in range(others):
        for i in range(count):
            k = i + 1 if (i - parity) % 2 == 0 else i - 1
            target = (k, j) if 0 <= k < count else (i, j ^ 1)
            if axis == "sy":
                pairs.append((i * nx + j, target[0] * nx + target[1]))
            else:
                pairs.append((j * nx + i, target[1] * nx + target[0]))
    return pairs


def swap(value, axis, parity):
    return lax.ppermute(value, ("sy", "sx"), swap_pairs(axis, parity))


CODES = 32767.0
STEPS = 8.0


def put_codes(send, pieces):
    length, width = pieces[0]().shape
    row = lax.broadcasted_iota(jnp.int32, (GROUP, width), 0)
    scales = jnp.zeros((GROUP, width), f32)
    for j, piece in enumerate(pieces):
        v = piece()
        top = jnp.max(jnp.max(jnp.abs(v), axis=0, keepdims=True), axis=1, keepdims=True)
        power = jnp.ceil(jnp.log2(jnp.maximum(top, 1e-12)) * STEPS) + 1.0
        t = v * (jnp.exp2(power * (-1.0 / STEPS)) * (CODES * CODES))
        code = t * lax.rsqrt(jnp.abs(t) + 1e-30)
        send[length * j : length * (j + 1), :] = to_int16(code)
        scales = jnp.where(row == j, power, scales)
    send[length * len(pieces) :, :] = to_int16(scales)


def to_int16(v):
    return jnp.round(v).astype(jnp.int32).astype(jnp.int16)


def get_codes(use_first, first, second, count, keep):
    length = (first.shape[0] - GROUP) // count

    def rows(start, size):
        both = jnp.where(use_first, first[start : start + size, :], second[start : start + size, :])
        return both.astype(jnp.int32).astype(f32)

    scale = jnp.exp2(rows(length * count, GROUP) * (1.0 / STEPS)) * (keep / (CODES * CODES))

    def piece(j):
        code = rows(length * j, length)
        return code * jnp.abs(code) * scale[j : j + 1, :]

    return piece


def lane_iota(shape):
    return lax.broadcasted_iota(jnp.int32, shape, len(shape) - 1)


def pack_rows_kernel(info, x, send_a, send_b, *, radius, first):
    frames, tile_rows, cols = x.shape[1:]
    rows = frames * radius
    even = info[0] == 0
    shape = (rows, frames * GROUP)
    r = lax.broadcasted_iota(jnp.int32, shape, 0)
    c = lax.broadcasted_iota(jnp.int32, shape, 1)
    base = (r // radius) * GROUP + r % radius
    sel_top = (c == base).astype(bf16)
    sel_bot = (c == base + (GROUP - radius)).astype(bf16)
    for n in range(send_a.shape[0]):
        up = x[first + n, :, :GROUP, :].reshape(frames * GROUP, cols)
        down = x[first + n, :, tile_rows - GROUP :, :].reshape(frames * GROUP, cols)
        up = jnp.dot(sel_top, up, preferred_element_type=f32).astype(bf16)
        down = jnp.dot(sel_bot, down, preferred_element_type=f32).astype(bf16)
        send_a[n] = jnp.where(even, down, up)
        send_b[n] = jnp.where(even, up, down)


def pack_rows(info, exposures, first, count, radius):
    nights, frames, rows, cols = exposures.shape
    out = jax.ShapeDtypeStruct((count, frames * radius, cols), bf16)
    return call(
        functools.partial(pack_rows_kernel, radius=radius, first=first),
        (out, out),
        [SMEM, VMEM],
        (info, exposures),
        flops=1 << 26,
        name="pack_rows",
    )


def pack_cols_kernel(info, x, row_a, row_b, send_a, send_b, *, radius, first):
    frames, rows, cols = x.shape[1:]
    even_y = info[0] == 0
    even_x = info[1] == 0
    lane = lane_iota((rows, LANES))
    halo_lane = lane_iota((frames * radius, LANES))
    for n in range(send_a.shape[0]):
        x_left = x[first + n, :, :, :LANES]
        x_right = x[first + n, :, :, cols - LANES :]
        la, lb = row_a[n, :, :LANES], row_b[n, :, :LANES]
        ra, rb = row_a[n, :, cols - LANES :], row_b[n, :, cols - LANES :]
        to_right = jnp.zeros((rows, LANES), bf16)
        to_left = jnp.zeros((rows, LANES), bf16)
        for e in range(frames):
            here = (lane >= radius * e) & (lane < radius * (e + 1))
            shift = (radius * (e + 1)) % LANES
            to_right = jnp.where(here, pltpu.roll(x_right[e], shift, 1), to_right)
            to_left = jnp.where(here, pltpu.roll(x_left[e], radius * e, 1), to_left)
        top_l = jnp.where(even_y, lb, la)
        bot_l = jnp.where(even_y, la, lb)
        top_r = jnp.where(even_y, rb, ra)
        bot_r = jnp.where(even_y, ra, rb)
        corner_right = jnp.where(
            halo_lane < radius, pltpu.roll(top_r, radius, 1), pltpu.roll(bot_r, 2 * radius, 1)
        )
        corner_left = jnp.where(halo_lane < radius, top_l, pltpu.roll(bot_l, radius, 1))
        send_a[n, :rows] = jnp.where(even_x, to_right, to_left)
        send_b[n, :rows] = jnp.where(even_x, to_left, to_right)
        send_a[n, rows:] = jnp.where(even_x, corner_right, corner_left)
        send_b[n, rows:] = jnp.where(even_x, corner_left, corner_right)


def pack_cols(info, exposures, recv, first, count, radius):
    nights, frames, rows, cols = exposures.shape
    out = jax.ShapeDtypeStruct((count, rows + frames * radius, LANES), bf16)
    return call(
        functools.partial(pack_cols_kernel, radius=radius, first=first),
        (out, out),
        [SMEM] + [VMEM] * 3,
        (info, exposures, *recv),
        flops=1 << 26,
        name="pack_cols",
    )


STRIDE = 3


def band_shape(rows, size):
    pitch = rows + 2 * GROUP
    count = -(-size // STRIDE)
    ring = -(-(pitch * count + 2 * GROUP) // LANES) * LANES
    return pitch, count, ring


def bands_kernel(psf, out, *, rows):
    nights, frames, size, _ = psf.shape
    radius = (size - 1) // 2
    pitch, count, ring = band_shape(rows, size)
    shape = (size, STRIDE * ring)
    b = lax.broadcasted_iota(jnp.int32, shape, 0)
    c = lax.broadcasted_iota(jnp.int32, shape, 1)
    at = c - (b % STRIDE) * ring
    total = jnp.zeros((nights * frames, STRIDE * ring), f32)
    for a in range(size):
        place = pitch * (b // STRIDE) + a - radius
        place = jnp.where(place < 0, place + ring, place)
        taps = jnp.concatenate([psf[n, :, a, :] for n in range(nights)], axis=0)
        total = total + jnp.dot(taps, (at == place).astype(bf16), preferred_element_type=f32)
    for e in range(nights * frames):
        for g in range(STRIDE):
            row = total[e : e + 1, ring * g : ring * (g + 1)]
            row = jnp.broadcast_to(row, (rows, ring))
            band = pltpu.roll(row, 0, 1, stride=1, stride_axis=0).astype(bf16)
            out[e // frames, e % frames, rows * g : rows * (g + 1), :] = band


def make_bands(psf_kernels, rows):
    nights, frames, size, _ = psf_kernels.shape
    pitch, count, ring = band_shape(rows, size)
    return call(
        functools.partial(bands_kernel, rows=rows),
        (jax.ShapeDtypeStruct((nights, frames, STRIDE * rows, ring), bf16),),
        [VMEM],
        (psf_kernels,),
        flops=1 << 28,
        name="make_bands",
        limit=24 << 20,
    )[0]


def filter_kernel(
    info, x, ra, rb, ca, cb, bands, out, border, image, windows, *, radius, night, half
):
    frames, rows, cols = x.shape[1], x.shape[2], x.shape[3]
    tiles = cols // LANES
    size = 2 * radius + 1
    pitch, count, ring = band_shape(rows, size)
    packed = frames * radius
    extra = pitch - rows
    even_y = info[0] == 0
    even_x = info[1] == 0
    zero = jnp.zeros((), bf16)
    top_ok = info[2] > 0
    bot_ok = info[2] < info[4] - 1
    left_ok = info[3] > 0
    right_ok = info[3] < info[5] - 1

    col_l = jnp.where(left_ok, jnp.where(even_x, cb[half], ca[half]), zero)
    col_r = jnp.where(right_ok, jnp.where(even_x, ca[half], cb[half]), zero)
    halo_lane = lane_iota((packed, LANES))
    corner_l, corner_r = col_l[rows:], col_r[rows:]
    side_top = jnp.where(
        halo_lane < radius,
        corner_r,
        jnp.where(halo_lane >= LANES - radius, pltpu.roll(corner_l, LANES - radius, 1), zero),
    )
    side_bot = jnp.where(
        halo_lane < radius,
        pltpu.roll(corner_r, LANES - radius, 1),
        jnp.where(halo_lane >= LANES - radius, pltpu.roll(corner_l, LANES - 2 * radius, 1), zero),
    )
    top = jnp.concatenate([jnp.where(even_y, rb[half], ra[half]), side_top], axis=1)
    bot = jnp.concatenate([jnp.where(even_y, ra[half], rb[half]), side_bot], axis=1)
    top = jnp.where(top_ok, top, zero)
    bot = jnp.where(bot_ok, bot, zero)
    top = pltpu.roll(top, cols + LANES - STRIDE, 1)
    shape = (frames * extra, packed)
    r = lax.broadcasted_iota(jnp.int32, shape, 0)
    c = lax.broadcasted_iota(jnp.int32, shape, 1)
    frame, place = r // extra, r % extra
    sel_bot = ((place < radius) & (c == frame * radius + place)).astype(bf16)
    from_top = place - (extra - radius)
    sel_top = ((from_top >= 0) & (c == frame * radius + from_top)).astype(bf16)
    border[...] = (
        jnp.dot(sel_bot, bot, preferred_element_type=f32)
        + jnp.dot(sel_top, top, preferred_element_type=f32)
    ).astype(bf16)

    lane = lane_iota((rows, LANES))
    lane_all = lane_iota((pitch, LANES))
    first = pitch * count
    last = ring - extra
    if last > first:
        windows[first:last, :] = jnp.zeros((last - first, cols + LANES), bf16)

    def turn(shift, source, mask_lane):
        if shift == 0:
            return source
        turned = [pltpu.roll(t, shift % LANES, 1) for t in source]
        size = len(source)
        if shift > 0:
            return [jnp.where(mask_lane < shift, turned[k - 1], turned[k]) for k in range(size)]
        return [
            jnp.where(mask_lane < LANES + shift, turned[k], turned[(k + 1) % size])
            for k in range(size)
        ]

    middle = (STRIDE - 1) // 2

    def one(e, carry):
        image[:rows, :cols] = x[night, e]
        side_r = pltpu.roll(col_r[:rows], (LANES - radius * e) % LANES, 1)
        side_l = pltpu.roll(col_l[:rows], (2 * LANES - radius - radius * e) % LANES, 1)
        image[:rows, cols:] = jnp.where(
            lane < radius, side_r, jnp.where(lane >= LANES - radius, side_l, zero)
        )
        image[rows:] = border[pl.ds(pl.multiple_of(e * extra, extra), extra)]
        parts = [image[:, LANES * k : LANES * (k + 1)] for k in range(tiles + 1)]
        for w in range(count):
            shift = radius - middle - STRIDE * w
            for k, value in enumerate(turn(shift, parts, lane_all)):
                windows[pitch * w : pitch * (w + 1), LANES * k : LANES * (k + 1)] = value
        tail = [t[rows:] for t in parts]
        for k, value in enumerate(turn(radius - middle + STRIDE, tail, lane_all[:extra])):
            windows[last:, LANES * k : LANES * (k + 1)] = value
        sums = jnp.dot(bands[night, e], windows[...], preferred_element_type=f32)
        total = None
        for g in range(STRIDE):
            part = sums[rows * g : rows * (g + 1)]
            part = [part[:, LANES * k : LANES * (k + 1)] for k in range(tiles + 1)]
            part = turn(middle - g, part, lane)
            total = part if total is None else [a + b for a, b in zip(total, part)]
        for k in range(tiles):
            out[e, :, LANES * k : LANES * (k + 1)] = total[k]
        return carry

    lax.fori_loop(0, frames, one, 0)


def filter_night(info, exposures, night, half, bands, rows_a, rows_b, cols_a, cols_b, radius):
    nights, frames, rows, cols = exposures.shape
    pitch, count, ring = band_shape(rows, 2 * radius + 1)
    return call(
        functools.partial(filter_kernel, radius=radius, night=night, half=half),
        (jax.ShapeDtypeStruct((frames, rows, cols), f32),),
        [SMEM] + [VMEM] * 6,
        (info, exposures, rows_a, rows_b, cols_a, cols_b, bands),
        scratch=[
            pltpu.VMEM((frames * 2 * GROUP, cols + LANES), bf16),
            pltpu.VMEM((pitch, cols + LANES), bf16),
            pltpu.VMEM((ring, cols + LANES), bf16),
        ],
        flops=2 * frames * STRIDE * rows * ring * cols,
        name="filter_night",
    )[0]


def row_strips(info, load, planes, margin, tile_rows, send_a, send_b):
    half = planes // 2
    odd = info[0]
    low = pl.multiple_of((tile_rows - margin) * (1 - odd), SUB)
    high = pl.multiple_of((tile_rows - margin) * odd, SUB)

    def piece(first, start, j):
        return lambda: load(first + j, pl.ds(start, margin))

    put_codes(send_a, [piece(half * odd, low, j) for j in range(half)])
    put_codes(send_b, [piece(half * (1 - odd), high, j) for j in range(half)])


def total_of(weights, night):
    total = weights[night, 0]
    for e in range(1, weights.shape[1]):
        total = total + weights[night, e]
    return total


def first_strips_kernel(info, weights, field, send_a, send_b, *, margin):
    planes, rows, cols = field.shape
    add = total_of(weights, 0)
    row_strips(info, lambda p, r: field[p, r, :] + add, planes, margin, rows, send_a, send_b)


def strip_shape(planes, length, width):
    return jax.ShapeDtypeStruct((planes // 2 * length + GROUP, width), jnp.int16)


def first_strips(info, weights, field):
    planes, rows, cols = field.shape
    margin = 3 * rows // 4
    out = strip_shape(planes, margin, cols)
    return call(
        functools.partial(first_strips_kernel, margin=margin),
        (out, out),
        [SMEM, SMEM, VMEM],
        (info, weights, field),
        flops=1 << 26,
        name="first_strips",
    )


def move_rows_kernel(
    info, offsets, weights, field, ra, rb, out, send_a, send_b, above, *, margin, side, night, grow
):
    planes, rows, cols = field.shape
    half = planes // 2
    even = info[0] == 0
    odd_x = info[1]
    top_ok = jnp.where(info[2] > 0, 1.0, 0.0)
    bot_ok = jnp.where(info[2] < info[4] - 1, 1.0, 0.0)
    sub = lax.broadcasted_iota(jnp.int32, (SUB, cols), 0)
    add = total_of(weights, night) if grow else None

    def turn(source, start):
        base = (start // SUB) * SUB
        rest = start % SUB
        back = (SUB - rest) % SUB
        keep = sub < SUB - rest
        turned = [
            pltpu.roll(source[pl.ds(pl.multiple_of(base + SUB * j, SUB), SUB), :], back, 0)
            for j in range(rows // SUB + 1)
        ]
        return [jnp.where(keep, turned[j], turned[j + 1]) for j in range(rows // SUB)]

    from_above = get_codes(even, rb, ra, half, top_ok)
    from_below = get_codes(even, ra, rb, half, bot_ok)
    for j in range(half):
        for p, got in ((j, from_above), (j + half, from_below)):
            source = above.at[p % above.shape[0]]
            own = field[p] + add if grow else field[p]
            if p < half:
                source[:margin] = got(j)
                source[margin : margin + rows] = own
                start = margin - offsets[night, p, 0]
            else:
                source[:rows] = own
                source[rows : rows + margin] = got(j)
                start = -offsets[night, p, 0]
            source[rows + margin :] = jnp.zeros((SUB, cols), f32)
            for k, value in enumerate(turn(source, start)):
                out[p, SUB * k : SUB * (k + 1), :] = value

    right = pl.multiple_of((cols - side) * (1 - odd_x), LANES)
    left = pl.multiple_of((cols - side) * odd_x, LANES)

    def piece(which, start, j):
        return lambda: out[2 * j + which, :, pl.ds(start, side)]

    put_codes(send_a, [piece(odd_x, right, j) for j in range(half)])
    put_codes(send_b, [piece(1 - odd_x, left, j) for j in range(half)])


def move_rows(info, offsets, weights, field, recv, night, grow):
    planes, rows, cols = field.shape
    margin = 3 * rows // 4
    side = 3 * cols // 4
    strip = strip_shape(planes, rows, side)
    return call(
        functools.partial(move_rows_kernel, margin=margin, side=side, night=night, grow=grow),
        (jax.ShapeDtypeStruct(field.shape, f32), strip, strip),
        [SMEM, SMEM, SMEM, VMEM, VMEM, VMEM],
        (info, offsets, weights, field, *recv),
        scratch=[pltpu.VMEM((planes, rows + margin + SUB, cols), f32)],
        flops=1 << 27,
        name="move_rows",
    )


def move_columns(info, offsets, night, field, ca, cb, out, wide, side):
    planes, rows, cols = field.shape
    half = planes // 2
    even = info[1] == 0
    left_ok = jnp.where(info[3] > 0, 1.0, 0.0)
    right_ok = jnp.where(info[3] < info[5] - 1, 1.0, 0.0)
    lane = lane_iota((rows, LANES))
    tiles = cols // LANES

    def turn(source, start):
        base = (start // LANES) * LANES
        rest = start % LANES
        back = (LANES - rest) % LANES
        keep = lane < LANES - rest
        turned = [
            pltpu.roll(source[:, pl.ds(pl.multiple_of(base + LANES * j, LANES), LANES)], back, 1)
            for j in range(tiles + 1)
        ]
        return [jnp.where(keep, turned[j], turned[j + 1]) for j in range(tiles)]

    from_left = get_codes(even, cb, ca, half, left_ok)
    from_right = get_codes(even, ca, cb, half, right_ok)
    for j in range(half):
        for p, got in ((2 * j, from_left), (2 * j + 1, from_right)):
            source = wide.at[p]
            if p % 2 == 0:
                source[:, :side] = got(j)
                source[:, side : side + cols] = field[p]
                start = side - offsets[night, p, 1]
            else:
                source[:, :cols] = field[p]
                source[:, cols : cols + side] = got(j)
                start = -offsets[night, p, 1]
            source[:, cols + side :] = jnp.zeros((rows, LANES), f32)
            for k, value in enumerate(turn(source, start)):
                out[p, :, LANES * k : LANES * (k + 1)] = value


def move_cols_kernel(info, offsets, weights, field, ca, cb, out, *rest, margin, side, night, more):
    planes, rows, cols = field.shape
    move_columns(info, offsets, night, field, ca, cb, out, rest[-1], side)
    if more:
        add = total_of(weights, night + 1)
        row_strips(
            info, lambda p, r: out[p, r, :] + add, planes, margin, rows, rest[0], rest[1]
        )


def move_cols(info, offsets, weights, field, recv, night, more):
    planes, rows, cols = field.shape
    margin = 3 * rows // 4
    side = 3 * cols // 4
    strips = (strip_shape(planes, margin, cols),) * (2 if more else 0)
    return call(
        functools.partial(move_cols_kernel, margin=margin, side=side, night=night, more=more),
        (jax.ShapeDtypeStruct(field.shape, f32),) + strips,
        [SMEM, SMEM, SMEM, VMEM, VMEM, VMEM],
        (info, offsets, weights, field, *recv),
        scratch=[pltpu.VMEM((planes, rows, cols + side + LANES), f32)],
        flops=1 << 27,
        name="move_cols",
    )


def stack_kernel(*refs, night, moved, last, margin, side):
    info, offsets, weights, flux, weight, filtered, masks = refs[:7]
    refs = refs[7:]
    if moved:
        ca, cb, *refs = refs
    out, out_1, *refs = refs
    if not last:
        out_2, *refs = refs
    table = refs[0]
    planes, rows, cols = flux.shape
    frames = filtered.shape[0]
    if moved:
        move_columns(info, offsets, night - 1, flux, ca, cb, out, refs[1], side)
    source = out if moved else flux
    tiles = cols // LANES
    lead = 2 if moved else 0
    grown = None
    for e in range(frames):
        gain = weights[night, e]
        if e >= lead:
            grown = gain if grown is None else grown + gain
        filled = jnp.full((SUB, LANES), gain, f32)
        table[0, e] = filled
        table[1, e] = band_scale / jnp.sqrt(filled)
        table[2, e] = jnp.full((SUB, LANES), 0.0 if grown is None else grown, f32)

    def chunk(i, carry):
        r = pl.ds(pl.multiple_of((i // tiles) * SUB, SUB), SUB)
        c = pl.ds(pl.multiple_of((i % tiles) * LANES, LANES), LANES)
        mean = [None] * planes
        held = [weight[p, r, c] for p in range(planes)]
        f = [source[p, r, c] for p in range(planes)]
        for e in range(frames):
            value = filtered[e, r, c]
            mask = masks[night, e, r, c]
            gain = table[0, e]
            band = table[1, e]
            grown = table[2, e]
            for p in range(planes):
                if e == lead:
                    if last:
                        out_1[p, r, c] = held[p] + table[2, frames - 1]
                    held[p] = jnp.maximum(held[p], weight_floor)
                    mean[p] = f[p] * pltpu.reciprocal(held[p], approx=True)
                if e < lead:
                    total = jnp.maximum(held[p], weight_floor)
                    mean[p] = f[p] * pltpu.reciprocal(total, approx=True)
                step = value - mean[p]
                clipped = jnp.minimum(jnp.maximum(step, -band), band)
                step = jnp.where((mask & (1 << p)) != 0, clipped, step)
                if e < lead:
                    f[p] = f[p] + gain * (mean[p] + step)
                    held[p] = held[p] + gain
                else:
                    part = gain * pltpu.reciprocal(held[p] + grown, approx=True)
                    mean[p] = mean[p] + part * step
        grown = table[2, frames - 1]
        for p in range(planes):
            out[p, r, c] = mean[p] * (held[p] + grown)
        return carry

    lax.fori_loop(0, (rows // SUB) * tiles, chunk, 0)
    if not last:
        row_strips(info, lambda p, r: out[p, r, :], planes, margin, rows, out_1, out_2)


def stack_night(info, offsets, weights, flux, weight, filtered, masks, night, recv, last):
    planes, rows, cols = flux.shape
    frames = masks.shape[1]
    margin = 3 * rows // 4
    side = 3 * cols // 4
    moved = recv is not None
    field = jax.ShapeDtypeStruct(flux.shape, f32)
    strip = strip_shape(planes, margin, cols)
    scratch = [pltpu.VMEM((3, frames, SUB, LANES), f32)]
    if moved:
        scratch.append(pltpu.VMEM((planes, rows, cols + side + LANES), f32))
    return call(
        functools.partial(
            stack_kernel, night=night, moved=moved, last=last, margin=margin, side=side
        ),
        (field, field) if last else (field, strip, strip),
        [SMEM] * 3 + [VMEM] * (6 if moved else 4),
        (info, offsets, weights, flux, weight, filtered, masks) + (tuple(recv) if moved else ()),
        scratch=scratch,
        flops=12 * frames * planes * rows * cols,
        name="stack_night",
    )


def per_device(
    exposures, psf_kernels, clip_masks, exposure_weights, plane_offsets, start_flux, start_weight
):
    nights, frames, rows, cols = exposures.shape
    radius = (psf_kernels.shape[2] - 1) // 2
    iy, ix = lax.axis_index("sy"), lax.axis_index("sx")
    ny, nx = lax.axis_size("sy"), lax.axis_size("sx")
    info = jnp.stack([iy % 2, ix % 2, iy, ix, jnp.int32(ny), jnp.int32(nx)]).astype(jnp.int32)

    halos = []
    for first, count in ((0, 1), (1, nights - 1)):
        sent = pack_rows(info, exposures, first, count, radius)
        got_rows = [swap(s, "sy", i) for i, s in enumerate(sent)]
        sent = pack_cols(info, exposures, got_rows, first, count, radius)
        got_cols = [swap(s, "sx", i) for i, s in enumerate(sent)]
        halos.append((got_rows, got_cols))
    bands = make_bands(psf_kernels, rows)

    def filtered(n):
        got_rows, got_cols = halos[min(n, 1)]
        half = 0 if n == 0 else n - 1
        return filter_night(info, exposures, n, half, bands, *got_rows, *got_cols, radius)

    weight = [start_weight]
    strips = first_strips(info, exposure_weights, start_weight)
    for n in range(nights - 1):
        got = [swap(s, "sy", i) for i, s in enumerate(strips)]
        moved, *sides = move_rows(
            info, plane_offsets, exposure_weights, weight[-1], got, n, True
        )
        got = [swap(s, "sx", i) for i, s in enumerate(sides)]
        new, *strips = move_cols(
            info, plane_offsets, exposure_weights, moved, got, n, n < nights - 2
        )
        weight.append(new)

    flux = start_flux
    recv = None
    for n in range(nights):
        last = n == nights - 1
        flux, *more = stack_night(
            info, plane_offsets, exposure_weights, flux, weight[n], filtered(n), clip_masks, n,
            recv, last,
        )
        if last:
            return flux, more[0]
        got = [swap(s, "sy", i) for i, s in enumerate(more)]
        flux, *sides = move_rows(info, plane_offsets, exposure_weights, flux, got, n, False)
        recv = [swap(s, "sx", i) for i, s in enumerate(sides)]


def solution(mesh):
    return jax.shard_map(
        per_device,
        mesh=mesh,
        in_specs=(
            P(None, None, "sy", "sx"),
            P(),
            P(None, None, "sy", "sx"),
            P(),
            P(),
            P(None, "sy", "sx"),
            P(None, "sy", "sx"),
        ),
        out_specs=(P(None, "sy", "sx"), P(None, "sy", "sx")),
        check_vma=False,
    )
```

```python
import functools
import math

import jax
import jax.numpy as jnp
from jax import lax
from jax.experimental import pallas as pl
from jax.experimental.pallas import tpu as pltpu
from jax.sharding import PartitionSpec as P

band_scale = 1.5
weight_floor = 1.0
LANES = 128
SUB = 8
GROUP = 16
bf16 = jnp.bfloat16
f32 = jnp.float32
SMEM = pl.BlockSpec(memory_space=pltpu.SMEM)
VMEM = pl.BlockSpec(memory_space=pltpu.VMEM)


def call(
    kernel, outs, in_specs, args, *, name, flops, scratch=(), limit=16 << 20, after=(),
    grid=(), out_specs=None, aliases=None,
):
    size = sum(math.prod(o.shape) * o.dtype.itemsize for o in outs)
    known = len(args)
    begin = known + len(after)
    end = begin + len(outs)
    token = jax.ShapeDtypeStruct((SUB, LANES), f32)

    def ordered(*refs):
        refs[end][...] = jnp.zeros((SUB, LANES), f32)
        kernel(*refs[:known], *refs[begin:end], *refs[end + 1 :])

    return pl.pallas_call(
        ordered,
        grid=grid,
        out_shape=(*outs, token),
        in_specs=list(in_specs) + [VMEM] * len(after),
        out_specs=(VMEM,) * (len(outs) + 1) if out_specs is None else (*out_specs, VMEM),
        scratch_shapes=list(scratch),
        input_output_aliases=aliases or {},
        compiler_params=pltpu.CompilerParams(vmem_limit_bytes=limit),
        cost_estimate=pl.CostEstimate(flops=flops, bytes_accessed=2 * size, transcendentals=0),
        name=name,
    )(*args, *after)


def swap_pairs(axis, parity):
    ny, nx = lax.axis_size("sy"), lax.axis_size("sx")
    count, others = (ny, nx) if axis == "sy" else (nx, ny)
    pairs = []
    for j in range(others):
        for i in range(count):
            k = i + 1 if (i - parity) % 2 == 0 else i - 1
            if axis == "sx":
                k %= count
            target = (k, j) if 0 <= k < count else (i, j ^ 1)
            if axis == "sy":
                pairs.append((i * nx + j, target[0] * nx + target[1]))
            else:
                pairs.append((j * nx + i, target[1] * nx + target[0]))
    return pairs


def swap(value, axis, parity):
    return lax.ppermute(value, ("sy", "sx"), swap_pairs(axis, parity))


def swap_rows(values):
    return [swap(v, "sy", parity) for parity, v in enumerate(values)]


def swap_columns(values):
    return [swap(v, "sx", parity) for parity, v in enumerate(values)]


CODES = 32767.0
STEPS = 8.0


def put_codes(send, pieces):
    length, width = pieces[0]().shape
    row = lax.broadcasted_iota(jnp.int32, (GROUP, width), 0)
    scales = jnp.zeros((GROUP, width), f32)
    for j, piece in enumerate(pieces):
        v = piece()
        top = jnp.max(jnp.max(jnp.abs(v), axis=0, keepdims=True), axis=1, keepdims=True)
        power = jnp.ceil(jnp.log2(jnp.maximum(top, 1e-12)) * STEPS) + 1.0
        t = v * (jnp.exp2(power * (-1.0 / STEPS)) * (CODES * CODES))
        code = t * lax.rsqrt(jnp.abs(t) + 1e-30)
        send[length * j : length * (j + 1), :] = to_int16(code)
        scales = jnp.where(row == j, power, scales)
    send[length * len(pieces) :, :] = to_int16(scales)


def to_int16(v):
    return v.astype(jnp.int32).astype(jnp.int16)


def get_codes(use_first, first, second, count, keep):
    length = (first.shape[0] - GROUP) // count

    def rows(start, size):
        both = jnp.where(use_first, first[start : start + size, :], second[start : start + size, :])
        return both.astype(jnp.int32).astype(f32)

    scale = jnp.exp2(rows(length * count, GROUP) * (1.0 / STEPS)) * (keep / (CODES * CODES))

    def piece(j):
        code = rows(length * j, length)
        return code * (jnp.abs(code) + 1.0) * scale[j : j + 1, :]

    return piece


def lane_iota(shape):
    return lax.broadcasted_iota(jnp.int32, shape, len(shape) - 1)


def pack_rows_kernel(info, x, send_a, send_b, *, radius, first):
    frames, tile_rows, cols = x.shape[1:]
    rows = frames * radius
    even = info[0] == 0
    shape = (rows, frames * GROUP)
    r = lax.broadcasted_iota(jnp.int32, shape, 0)
    c = lax.broadcasted_iota(jnp.int32, shape, 1)
    base = (r // radius) * GROUP + r % radius
    sel_top = (c == base).astype(bf16)
    sel_bot = (c == base + (GROUP - radius)).astype(bf16)
    for n in range(send_a.shape[0]):
        up = x[first + n, :, :GROUP, :].reshape(frames * GROUP, cols)
        down = x[first + n, :, tile_rows - GROUP :, :].reshape(frames * GROUP, cols)
        up = jnp.dot(sel_top, up, preferred_element_type=f32).astype(bf16)
        down = jnp.dot(sel_bot, down, preferred_element_type=f32).astype(bf16)
        send_a[n] = jnp.where(even, down, up)
        send_b[n] = jnp.where(even, up, down)


def pack_rows(info, exposures, first, count, radius, after=()):
    nights, frames, rows, cols = exposures.shape
    out = jax.ShapeDtypeStruct((count, frames * radius, cols), bf16)
    return call(
        functools.partial(pack_rows_kernel, radius=radius, first=first),
        (out, out),
        [SMEM, VMEM],
        (info, exposures),
        flops=1 << 26,
        name="pack_rows",
        after=after,
    )


def pack_cols_kernel(info, x, row_a, row_b, send_a, send_b, *, radius, first):
    frames, rows, cols = x.shape[1:]
    even_y = info[0] == 0
    even_x = info[1] == 0
    lane = lane_iota((rows, LANES))
    halo_lane = lane_iota((frames * radius, LANES))
    for n in range(send_a.shape[0]):
        x_left = x[first + n, :, :, :LANES]
        x_right = x[first + n, :, :, cols - LANES :]
        la, lb = row_a[n, :, :LANES], row_b[n, :, :LANES]
        ra, rb = row_a[n, :, cols - LANES :], row_b[n, :, cols - LANES :]
        to_right = jnp.zeros((rows, LANES), bf16)
        to_left = jnp.zeros((rows, LANES), bf16)
        for e in range(frames):
            here = (lane >= radius * e) & (lane < radius * (e + 1))
            shift = (radius * (e + 1)) % LANES
            to_right = jnp.where(here, pltpu.roll(x_right[e], shift, 1), to_right)
            to_left = jnp.where(here, pltpu.roll(x_left[e], radius * e, 1), to_left)
        top_l = jnp.where(even_y, lb, la)
        bot_l = jnp.where(even_y, la, lb)
        top_r = jnp.where(even_y, rb, ra)
        bot_r = jnp.where(even_y, ra, rb)
        corner_right = jnp.where(
            halo_lane < radius, pltpu.roll(top_r, radius, 1), pltpu.roll(bot_r, 2 * radius, 1)
        )
        corner_left = jnp.where(halo_lane < radius, top_l, pltpu.roll(bot_l, radius, 1))
        send_a[n, :rows] = jnp.where(even_x, to_right, to_left)
        send_b[n, :rows] = jnp.where(even_x, to_left, to_right)
        send_a[n, rows:] = jnp.where(even_x, corner_right, corner_left)
        send_b[n, rows:] = jnp.where(even_x, corner_left, corner_right)


def pack_cols(info, exposures, recv, first, count, radius, after=()):
    nights, frames, rows, cols = exposures.shape
    out = jax.ShapeDtypeStruct((count, rows + frames * radius, LANES), bf16)
    return call(
        functools.partial(pack_cols_kernel, radius=radius, first=first),
        (out, out),
        [SMEM] + [VMEM] * 3,
        (info, exposures, *recv),
        flops=1 << 26,
        after=after,
        name="pack_cols",
    )


STRIDE = 3


def band_shape(rows, size):
    pitch = rows + 2 * GROUP
    count = -(-size // STRIDE)
    ring = -(-(pitch * count + 2 * GROUP) // LANES) * LANES
    return pitch, count, ring


def bands_kernel(psf, out, *, rows):
    _, size, frames, _ = psf.shape
    nights = out.shape[0]
    radius = (size - 1) // 2
    pitch, count, ring = band_shape(rows, size)
    shape = (size, STRIDE * ring)
    b = lax.broadcasted_iota(jnp.int32, shape, 0)
    c = lax.broadcasted_iota(jnp.int32, shape, 1)
    key = c - (b % STRIDE) * ring - pitch * (b // STRIDE) + radius
    key = jnp.where(key >= ring, key - ring, key)
    key = jnp.where(c // ring == b % STRIDE, key, -1)
    total = jnp.zeros((nights * frames, STRIDE * ring), f32)
    for a in range(size):
        taps = jnp.concatenate([psf[n, a] for n in range(nights)], axis=0)
        total = total + jnp.dot(taps, (key == a).astype(bf16), preferred_element_type=f32)
    for e in range(nights * frames):
        for g in range(STRIDE):
            row = total[e : e + 1, ring * g : ring * (g + 1)]
            row = jnp.broadcast_to(row, (rows, ring))
            band = pltpu.roll(row, 0, 1, stride=1, stride_axis=0).astype(bf16)
            out[e // frames, e % frames, rows * g : rows * (g + 1), :] = band


def make_bands(psf_kernels, rows, after):
    nights, frames, size, _ = psf_kernels.shape
    ring = band_shape(rows, size)[2]
    return call(
        functools.partial(bands_kernel, rows=rows),
        (jax.ShapeDtypeStruct((nights, frames, STRIDE * rows, ring), bf16),),
        [VMEM],
        (jnp.swapaxes(psf_kernels, 1, 2),),
        flops=1 << 28,
        name="make_bands",
        limit=24 << 20,
        after=after,
    )


def filter_kernel(
    info, x, ra, rb, ca, cb, bands, out, border, image_0, image_1, windows_0, windows_1,
    *, radius, night, half, start
):
    frames, rows, cols = out.shape
    tiles = cols // LANES
    size = 2 * radius + 1
    pitch, count, ring = band_shape(rows, size)
    packed = ra.shape[1]
    extra = pitch - rows
    even_y = info[0] == 0
    even_x = info[1] == 0
    zero = jnp.zeros((), bf16)
    top_ok = info[2] > 0
    bot_ok = info[2] < info[4] - 1
    left_ok = info[3] > 0
    right_ok = info[3] < info[5] - 1

    col_l = jnp.where(left_ok, jnp.where(even_x, cb[half], ca[half]), zero)
    col_r = jnp.where(right_ok, jnp.where(even_x, ca[half], cb[half]), zero)
    halo_lane = lane_iota((packed, LANES))
    corner_l, corner_r = col_l[rows:], col_r[rows:]
    side_top = jnp.where(
        halo_lane < radius,
        corner_r,
        jnp.where(halo_lane >= LANES - radius, pltpu.roll(corner_l, LANES - radius, 1), zero),
    )
    side_bot = jnp.where(
        halo_lane < radius,
        pltpu.roll(corner_r, LANES - radius, 1),
        jnp.where(halo_lane >= LANES - radius, pltpu.roll(corner_l, LANES - 2 * radius, 1), zero),
    )
    top = jnp.concatenate([jnp.where(even_y, rb[half], ra[half]), side_top], axis=1)
    bot = jnp.concatenate([jnp.where(even_y, ra[half], rb[half]), side_bot], axis=1)
    top = jnp.where(top_ok, top, zero)
    bot = jnp.where(bot_ok, bot, zero)
    top = pltpu.roll(top, cols + LANES - STRIDE, 1)
    shape = (frames * extra, packed)
    r = lax.broadcasted_iota(jnp.int32, shape, 0)
    c = lax.broadcasted_iota(jnp.int32, shape, 1)
    frame, place = r // extra + start, r % extra
    sel_bot = ((place < radius) & (c == frame * radius + place)).astype(bf16)
    from_top = place - (extra - radius)
    sel_top = ((from_top >= 0) & (c == frame * radius + from_top)).astype(bf16)
    border[...] = (
        jnp.dot(sel_bot, bot, preferred_element_type=f32)
        + jnp.dot(sel_top, top, preferred_element_type=f32)
    ).astype(bf16)

    lane = lane_iota((rows, LANES))
    lane_all = lane_iota((pitch, LANES))
    first = pitch * count
    last = ring - extra
    if last > first:
        for windows in (windows_0, windows_1):
            windows[first:last, :] = jnp.zeros((last - first, cols + LANES), bf16)

    def turn(shift, source, mask_lane):
        if shift == 0:
            return source
        turned = [pltpu.roll(t, shift % LANES, 1) for t in source]
        size = len(source)
        if shift > 0:
            return [jnp.where(mask_lane < shift, turned[k - 1], turned[k]) for k in range(size)]
        return [
            jnp.where(mask_lane < LANES + shift, turned[k], turned[(k + 1) % size])
            for k in range(size)
        ]

    middle = (STRIDE - 1) // 2

    def prepare(e, image, windows):
        image[:rows, :cols] = x[night, start + e]
        side_r = pltpu.roll(col_r[:rows], (LANES - radius * (start + e)) % LANES, 1)
        side_l = pltpu.roll(col_l[:rows], (2 * LANES - radius - radius * (start + e)) % LANES, 1)
        image[:rows, cols:] = jnp.where(
            lane < radius, side_r, jnp.where(lane >= LANES - radius, side_l, zero)
        )
        image[rows:] = border[pl.ds(pl.multiple_of(e * extra, extra), extra)]
        parts = [image[:, LANES * k : LANES * (k + 1)] for k in range(tiles + 1)]
        for w in range(count):
            shift = radius - middle - STRIDE * w
            for k, value in enumerate(turn(shift, parts, lane_all)):
                windows[pitch * w : pitch * (w + 1), LANES * k : LANES * (k + 1)] = value
        tail = [t[rows:] for t in parts]
        for k, value in enumerate(turn(radius - middle + STRIDE, tail, lane_all[:extra])):
            windows[last:, LANES * k : LANES * (k + 1)] = value

    def combine(e, windows):
        sums = jnp.dot(bands[night, start + e], windows[...], preferred_element_type=f32)
        total = None
        for g in range(STRIDE):
            part = sums[rows * g : rows * (g + 1)]
            part = [part[:, LANES * k : LANES * (k + 1)] for k in range(tiles + 1)]
            part = turn(middle - g, part, lane)
            total = part if total is None else [a + b for a, b in zip(total, part)]
        for k in range(tiles):
            out[e, :, LANES * k : LANES * (k + 1)] = total[k]

    def pair(i, carry):
        prepare(2 * i + 1, image_1, windows_1)
        combine(2 * i, windows_0)
        prepare(jnp.minimum(2 * i + 2, frames - 1), image_0, windows_0)
        combine(2 * i + 1, windows_1)
        return carry

    prepare(0, image_0, windows_0)
    lax.fori_loop(0, frames // 2, pair, 0)
    if frames % 2:
        combine(frames - 1, windows_0)


def filter_night(
    info, exposures, night, half, bands, got_rows, got_cols, start, count, radius, after
):
    nights, frames, rows, cols = exposures.shape
    pitch, _, ring = band_shape(rows, 2 * radius + 1)
    return call(
        functools.partial(filter_kernel, radius=radius, night=night, half=half, start=start),
        (jax.ShapeDtypeStruct((count, rows, cols), f32),),
        [SMEM] + [VMEM] * 6,
        (info, exposures, *got_rows, *got_cols, bands),
        scratch=[
            pltpu.VMEM((count * 2 * GROUP, cols + LANES), bf16),
            pltpu.VMEM((pitch, cols + LANES), bf16),
            pltpu.VMEM((pitch, cols + LANES), bf16),
            pltpu.VMEM((ring, cols + LANES), bf16),
            pltpu.VMEM((ring, cols + LANES), bf16),
        ],
        after=after,
        flops=2 * count * STRIDE * rows * ring * cols,
        name="filter_night",
    )


QUAD = 4
FIELDS = 2 * QUAD
DOWN, UP = (0, 1, 4, 5), (2, 3, 6, 7)
RIGHT, LEFT = (0, 2, 4, 6), (1, 3, 5, 7)


def plane_of(group, q, planes):
    return (q // 2) * (planes // 2) + 2 * group + q % 2


def strip_shape(length, width):
    return jax.ShapeDtypeStruct((len(DOWN) * length + GROUP, width), jnp.int16)


def put_sides(odd, source, first_way, second_way, axis, margin, sends):
    size = source.shape[axis]
    end = pl.multiple_of((size - margin) * (1 - odd), SUB if axis == 1 else LANES)
    begin = pl.multiple_of((size - margin) * odd, SUB if axis == 1 else LANES)
    for send, start, swapped in ((sends[0], end, odd), (sends[1], begin, 1 - odd)):
        cut = pl.ds(start, margin)

        def piece(a, b, cut=cut, swapped=swapped):
            f = a + (b - a) * swapped
            return lambda: source[f, cut, :] if axis == 1 else source[f, :, cut]

        put_codes(send, [piece(a, b) for a, b in zip(first_way, second_way)])


def move_rows_kernel(
    info, offsets, field, ra, rb, out, send_a, send_b, above, *, margin, side, night, planes
):
    group_planes, group = planes
    fields, rows, cols = field.shape
    even = info[0] == 0
    top_ok = jnp.where(info[2] > 0, 1.0, 0.0)
    bot_ok = jnp.where(info[2] < info[4] - 1, 1.0, 0.0)
    sub = lax.broadcasted_iota(jnp.int32, (SUB, cols), 0)

    def turn(source, start):
        base = (start // SUB) * SUB
        rest = start % SUB
        back = (SUB - rest) % SUB
        keep = sub < SUB - rest
        turned = [
            pltpu.roll(source[pl.ds(pl.multiple_of(base + SUB * j, SUB), SUB), :], back, 0)
            for j in range(rows // SUB + 1)
        ]
        return [jnp.where(keep, turned[j], turned[j + 1]) for j in range(rows // SUB)]

    from_above = get_codes(even, rb, ra, len(DOWN), top_ok)
    from_below = get_codes(even, ra, rb, len(UP), bot_ok)
    for j in range(len(DOWN)):
        for f, got in ((DOWN[j], from_above), (UP[j], from_below)):
            source = above.at[f]
            offset = offsets[night, 0, plane_of(group, f % QUAD, group_planes)]
            if f in DOWN:
                source[:margin] = got(j)
                source[margin : margin + rows] = field[f]
                start = margin - offset
            else:
                source[:rows] = field[f]
                source[rows : rows + margin] = got(j)
                start = -offset
            source[rows + margin :] = jnp.zeros((SUB, cols), f32)
            for k, value in enumerate(turn(source, start)):
                out[f, SUB * k : SUB * (k + 1), :] = value
    put_sides(info[1], out, RIGHT, LEFT, 2, side, (send_a, send_b))


def move_rows(info, offsets, field, recv, night, planes, after):
    fields, rows, cols = field.shape
    margin = 3 * rows // 4
    side = 3 * cols // 4
    strip = strip_shape(rows, side)
    return call(
        functools.partial(
            move_rows_kernel, margin=margin, side=side, night=night, planes=planes
        ),
        (jax.ShapeDtypeStruct(field.shape, f32), strip, strip),
        [SMEM, SMEM, VMEM, VMEM, VMEM],
        (info, offsets, field, *recv),
        scratch=[pltpu.VMEM((fields, rows + margin + SUB, cols), f32)],
        flops=1 << 27,
        after=after,
        name="move_rows",
    )


def move_columns(info, offsets, night, field, ca, cb, out, wide, side, planes):
    group_planes, group = planes
    fields, rows, cols = field.shape
    even = info[1] == 0
    left_ok = jnp.where(info[3] > 0, 1.0, 0.0)
    right_ok = jnp.where(info[3] < info[5] - 1, 1.0, 0.0)
    lane = lane_iota((rows, LANES))
    tiles = cols // LANES

    def turn(source, start):
        base = (start // LANES) * LANES
        rest = start % LANES
        back = (LANES - rest) % LANES
        keep = lane < LANES - rest
        turned = [
            pltpu.roll(source[:, pl.ds(pl.multiple_of(base + LANES * j, LANES), LANES)], back, 1)
            for j in range(tiles + 1)
        ]
        return [jnp.where(keep, turned[j], turned[j + 1]) for j in range(tiles)]

    from_left = get_codes(even, cb, ca, len(RIGHT), left_ok)
    from_right = get_codes(even, ca, cb, len(LEFT), right_ok)
    for j in range(len(RIGHT)):
        for f, got in ((RIGHT[j], from_left), (LEFT[j], from_right)):
            source = wide.at[f]
            offset = offsets[night, 1, plane_of(group, f % QUAD, group_planes)]
            if f in RIGHT:
                source[:, :side] = got(j)
                source[:, side : side + cols] = field[f]
                start = side - offset
            else:
                source[:, :cols] = field[f]
                source[:, cols : cols + side] = got(j)
                start = -offset
            source[:, cols + side :] = jnp.zeros((rows, LANES), f32)
            for k, value in enumerate(turn(source, start)):
                out[f, :, LANES * k : LANES * (k + 1)] = value


def stack_kernel(*refs, night, last, margin, side, planes, parts, spare):
    info, offsets, weights, masks, *refs = refs
    images, refs = refs[:parts], refs[parts:]
    filtered = [part.at[e] for part in images for e in range(part.shape[0])]
    moved = night > 0
    group_planes, group = planes
    if moved:
        field, ca, cb, *refs = refs
        _, rows, cols = field.shape
    else:
        start_flux, start_weight, *refs = refs
        rows, cols = start_flux.shape[1:]
    refs = refs[spare:]
    if last:
        out_flux, out_weight, *refs = refs
    else:
        out, send_a, send_b, *refs = refs
    table = refs[0]
    frames = len(filtered)
    tiles = cols // LANES
    lead = 2 if moved else 0

    def prepare():
        if moved:
            move_columns(
                info, offsets, night - 1, field, ca, cb, refs[2], refs[1], side, planes
            )
        grown = None
        for e in range(frames):
            gain = weights[night, e]
            if e >= lead:
                grown = gain if grown is None else grown + gain
            filled = jnp.full((SUB, LANES), gain, f32)
            band = band_scale / jnp.sqrt(filled)
            table[0, e] = filled
            table[1, e] = band
            table[2, e] = -band
            table[3, e] = jnp.full((SUB, LANES), 0.0 if grown is None else grown, f32)

    def chunk(r, c, o):
        mean = [None] * QUAD
        after = [None] * QUAD
        ids = [plane_of(group, q, group_planes) for q in range(QUAD)]
        if moved:
            f = [refs[2][q, r, c] for q in range(QUAD)]
            held = [refs[2][QUAD + q, r, c] for q in range(QUAD)]
        else:
            f = [start_flux[p, r, c] for p in ids]
            held = [start_weight[p, r, c] for p in ids]
        for e in range(frames):
            value = filtered[e][r, c]
            mask = masks[night, e, r, c]
            gain, above, below, grown = (table[k, e] for k in range(4))
            for q in range(QUAD):
                if e == lead:
                    after[q] = held[q] + table[3, frames - 1]
                    held[q] = jnp.maximum(held[q], weight_floor)
                    mean[q] = f[q] * pltpu.reciprocal(held[q], approx=True)
                if e < lead:
                    total = jnp.maximum(held[q], weight_floor)
                    mean[q] = f[q] * pltpu.reciprocal(total, approx=True)
                step = value - mean[q]
                clipped = jnp.minimum(jnp.maximum(step, below), above)
                step = jnp.where((mask & (1 << ids[q])) != 0, clipped, step)
                if e < lead:
                    f[q] = f[q] + gain * (mean[q] + step)
                    held[q] = held[q] + gain
                else:
                    part = gain * pltpu.reciprocal(held[q] + grown, approx=True)
                    mean[q] = mean[q] + part * step
        grown = table[3, frames - 1]
        for q in range(QUAD):
            flux = mean[q] * (held[q] + grown)
            if last:
                out_flux[q // 2, 0, q % 2, o, c] = flux
                out_weight[q // 2, 0, q % 2, o, c] = after[q]
            else:
                out[q, o, c] = flux
                out[QUAD + q, o, c] = after[q]

    def cut(i, size):
        return pl.ds(pl.multiple_of(i * size, size), size)

    if last:
        i = pl.program_id(0)
        pl.when(i == 0)(prepare)

        @pl.loop(0, tiles)
        def _(k):
            chunk(cut(i, SUB), cut(k, LANES), pl.ds(0, SUB))
    else:
        prepare()

        @pl.loop(0, rows // SUB * tiles)
        def _(k):
            chunk(cut(k // tiles, SUB), cut(k % tiles, LANES), cut(k // tiles, SUB))

        put_sides(info[0], out, DOWN, UP, 1, margin, (send_a, send_b))


def stack_night(info, offsets, weights, masks, images, state, night, planes, earlier, after):
    nights, frames, rows, cols = masks.shape
    margin = 3 * rows // 4
    side = 3 * cols // 4
    last = night == nights - 1
    scratch = [pltpu.VMEM((4, frames, SUB, LANES), f32)]
    if night > 0:
        scratch.append(pltpu.VMEM((FIELDS, rows, cols + side + LANES), f32))
        scratch.append(pltpu.VMEM((FIELDS, rows, cols), f32))
    args = (info, offsets, weights, masks, *images, *state)
    specs = [SMEM] * 3 + [VMEM] * (len(args) - 3)
    kernel = functools.partial(
        stack_kernel, night=night, last=last, margin=margin, side=side, planes=planes,
        parts=len(images), spare=len(earlier),
    )
    known = dict(
        scratch=scratch,
        flops=12 * frames * QUAD * rows * cols,
        name="stack_night",
        after=after,
    )
    if not last:
        strip = strip_shape(margin, cols)
        out = jax.ShapeDtypeStruct((FIELDS, rows, cols), f32)
        return call(kernel, (out, strip, strip), specs, args, **known)
    total, group = planes
    out = jax.ShapeDtypeStruct((2, total // QUAD, 2, rows, cols), f32)
    block = pl.BlockSpec((2, 1, 2, SUB, cols), lambda i: (0, group, 0, i, 0))
    return call(
        kernel,
        (out, out),
        specs + [pl.BlockSpec(memory_space=pl.ANY)] * len(earlier),
        (*args, *earlier),
        grid=(rows // SUB,),
        out_specs=(block, block),
        aliases={len(args) + i: i for i in range(len(earlier))},
        **known,
    )


def per_device(
    exposures, psf_kernels, clip_masks, exposure_weights, plane_offsets, start_flux, start_weight
):
    nights, frames, rows, cols = exposures.shape
    planes_total = start_flux.shape[0]
    radius = (psf_kernels.shape[2] - 1) // 2
    iy, ix = lax.axis_index("sy"), lax.axis_index("sx")
    ny, nx = lax.axis_size("sy"), lax.axis_size("sx")
    info = jnp.stack([iy % 2, ix % 2, iy, ix, jnp.int32(ny), jnp.int32(nx)]).astype(jnp.int32)

    offsets = jnp.swapaxes(plane_offsets, 1, 2)

    *sent, done = pack_rows(info, exposures, 0, 1, radius)
    rows_first = swap_rows(sent)
    bands, done = make_bands(psf_kernels, rows, (done,))
    *sent, done = pack_cols(info, exposures, rows_first, 0, 1, radius, (done,))
    cols_first = swap_columns(sent)
    *sent, done = pack_rows(info, exposures, 1, nights - 1, radius, (done,))
    rows_later = swap_rows(sent)
    image, done = filter_night(
        info, exposures, 0, 0, bands, rows_first, cols_first, 0, frames, radius, (done,)
    )

    groups = [(planes_total, g) for g in range(planes_total // QUAD)]
    states = [(start_flux, start_weight)] * len(groups)
    results = ()
    for n in range(nights):
        fields = []
        sent = []
        for group, state in zip(groups, states):
            first, *strips, done = stack_night(
                info, offsets, exposure_weights, clip_masks, (image,), state, n, group, results,
                (done,),
            )
            fields.append(first)
            if n == nights - 1:
                results = (first, *strips)
            else:
                sent.append(swap_rows(strips))
        if n == nights - 1:
            shape = (planes_total, rows, cols)
            return tuple(r.reshape(shape) for r in results)
        if n == 0:
            *later, done = pack_cols(info, exposures, rows_later, 1, nights - 1, radius, (done,))
            cols_later = swap_columns(later)
        states = []
        for i, group in enumerate(groups):
            field, *strips, done = move_rows(
                info, offsets, fields[i], sent[i], n, group, (done,)
            )
            states.append((field, *swap_columns(strips)))
            if i == 0:
                image, done = filter_night(
                    info, exposures, n + 1, n, bands, rows_later, cols_later, 0, frames, radius,
                    (done,),
                )


def solution(mesh):
    return jax.shard_map(
        per_device,
        mesh=mesh,
        in_specs=(
            P(None, None, "sy", "sx"),
            P(),
            P(None, None, "sy", "sx"),
            P(),
            P(),
            P(None, "sy", "sx"),
            P(None, "sy", "sx"),
        ),
        out_specs=(P(None, "sy", "sx"), P(None, "sy", "sx")),
        check_vma=False,
    )
```

```python
import functools
import math

import jax
import jax.numpy as jnp
from jax import lax
from jax.experimental import pallas as pl
from jax.experimental.pallas import tpu as pltpu
from jax.sharding import PartitionSpec as P

band_scale = 1.5
weight_floor = 1.0
LANES = 128
SUB = 8
GROUP = 16
bf16 = jnp.bfloat16
f32 = jnp.float32
SMEM = pl.BlockSpec(memory_space=pltpu.SMEM)
VMEM = pl.BlockSpec(memory_space=pltpu.VMEM)


def call(
    kernel, outs, in_specs, args, *, name, flops, scratch=(), limit=16 << 20, after=(),
    grid=(), out_specs=None, aliases=None,
):
    size = sum(math.prod(o.shape) * o.dtype.itemsize for o in outs)
    known = len(args)
    begin = known + len(after)
    end = begin + len(outs)
    token = jax.ShapeDtypeStruct((SUB, LANES), f32)

    def ordered(*refs):
        refs[end][...] = jnp.zeros((SUB, LANES), f32)
        kernel(*refs[:known], *refs[begin:end], *refs[end + 1 :])

    return pl.pallas_call(
        ordered,
        grid=grid,
        out_shape=(*outs, token),
        in_specs=list(in_specs) + [VMEM] * len(after),
        out_specs=(VMEM,) * (len(outs) + 1) if out_specs is None else (*out_specs, VMEM),
        scratch_shapes=list(scratch),
        input_output_aliases=aliases or {},
        compiler_params=pltpu.CompilerParams(vmem_limit_bytes=limit),
        cost_estimate=pl.CostEstimate(flops=flops, bytes_accessed=2 * size, transcendentals=0),
        name=name,
    )(*args, *after)


def swap_pairs(axis, parity):
    ny, nx = lax.axis_size("sy"), lax.axis_size("sx")
    count, others = (ny, nx) if axis == "sy" else (nx, ny)
    pairs = []
    for j in range(others):
        for i in range(count):
            k = i + 1 if (i - parity) % 2 == 0 else i - 1
            if axis == "sx":
                k %= count
            target = (k, j) if 0 <= k < count else (i, j ^ 1)
            if axis == "sy":
                pairs.append((i * nx + j, target[0] * nx + target[1]))
            else:
                pairs.append((j * nx + i, target[1] * nx + target[0]))
    return pairs


def swap(value, axis, parity):
    return lax.ppermute(value, ("sy", "sx"), swap_pairs(axis, parity))


def swap_rows(values):
    return [swap(v, "sy", parity) for parity, v in enumerate(values)]


def swap_columns(values):
    return [swap(v, "sx", parity) for parity, v in enumerate(values)]


CODES = 32767.0
STEPS = 8.0


def put_codes(send, pieces):
    length, width = pieces[0]().shape
    row = lax.broadcasted_iota(jnp.int32, (GROUP, width), 0)
    scales = jnp.zeros((GROUP, width), f32)
    for j, piece in enumerate(pieces):
        v = piece()
        top = jnp.max(jnp.max(jnp.abs(v), axis=0, keepdims=True), axis=1, keepdims=True)
        power = jnp.ceil(jnp.log2(jnp.maximum(top, 1e-12)) * STEPS) + 1.0
        t = v * (jnp.exp2(power * (-1.0 / STEPS)) * (CODES * CODES))
        code = t * lax.rsqrt(jnp.abs(t) + 1e-30)
        send[length * j : length * (j + 1), :] = to_int16(code)
        scales = jnp.where(row == j, power, scales)
    send[length * len(pieces) :, :] = to_int16(scales)


def to_int16(v):
    return v.astype(jnp.int32).astype(jnp.int16)


def get_codes(use_first, first, second, count, keep):
    length = (first.shape[0] - GROUP) // count

    def rows(start, size):
        both = jnp.where(use_first, first[start : start + size, :], second[start : start + size, :])
        return both.astype(jnp.int32).astype(f32)

    scale = jnp.exp2(rows(length * count, GROUP) * (1.0 / STEPS)) * (keep / (CODES * CODES))

    def piece(j):
        code = rows(length * j, length)
        return code * (jnp.abs(code) + 1.0) * scale[j : j + 1, :]

    return piece


def lane_iota(shape):
    return lax.broadcasted_iota(jnp.int32, shape, len(shape) - 1)


def pack_rows_kernel(info, x, send_a, send_b, *, radius, first):
    frames, tile_rows, cols = x.shape[1:]
    rows = frames * radius
    even = info[0] == 0
    shape = (rows, frames * GROUP)
    r = lax.broadcasted_iota(jnp.int32, shape, 0)
    c = lax.broadcasted_iota(jnp.int32, shape, 1)
    base = (r // radius) * GROUP + r % radius
    sel_top = (c == base).astype(bf16)
    sel_bot = (c == base + (GROUP - radius)).astype(bf16)
    for n in range(send_a.shape[0]):
        up = x[first + n, :, :GROUP, :].reshape(frames * GROUP, cols)
        down = x[first + n, :, tile_rows - GROUP :, :].reshape(frames * GROUP, cols)
        up = jnp.dot(sel_top, up, preferred_element_type=f32).astype(bf16)
        down = jnp.dot(sel_bot, down, preferred_element_type=f32).astype(bf16)
        send_a[n] = jnp.where(even, down, up)
        send_b[n] = jnp.where(even, up, down)


def pack_rows(info, exposures, first, count, radius, after=()):
    nights, frames, rows, cols = exposures.shape
    out = jax.ShapeDtypeStruct((count, frames * radius, cols), bf16)
    return call(
        functools.partial(pack_rows_kernel, radius=radius, first=first),
        (out, out),
        [SMEM, VMEM],
        (info, exposures),
        flops=1 << 26,
        name="pack_rows",
        after=after,
    )


def pack_cols_kernel(info, x, row_a, row_b, send_a, send_b, *, radius, first):
    frames, rows, cols = x.shape[1:]
    even_y = info[0] == 0
    even_x = info[1] == 0
    lane = lane_iota((rows, LANES))
    halo_lane = lane_iota((frames * radius, LANES))
    for n in range(send_a.shape[0]):
        x_left = x[first + n, :, :, :LANES]
        x_right = x[first + n, :, :, cols - LANES :]
        la, lb = row_a[n, :, :LANES], row_b[n, :, :LANES]
        ra, rb = row_a[n, :, cols - LANES :], row_b[n, :, cols - LANES :]
        to_right = jnp.zeros((rows, LANES), bf16)
        to_left = jnp.zeros((rows, LANES), bf16)
        for e in range(frames):
            here = (lane >= radius * e) & (lane < radius * (e + 1))
            shift = (radius * (e + 1)) % LANES
            to_right = jnp.where(here, pltpu.roll(x_right[e], shift, 1), to_right)
            to_left = jnp.where(here, pltpu.roll(x_left[e], radius * e, 1), to_left)
        top_l = jnp.where(even_y, lb, la)
        bot_l = jnp.where(even_y, la, lb)
        top_r = jnp.where(even_y, rb, ra)
        bot_r = jnp.where(even_y, ra, rb)
        corner_right = jnp.where(
            halo_lane < radius, pltpu.roll(top_r, radius, 1), pltpu.roll(bot_r, 2 * radius, 1)
        )
        corner_left = jnp.where(halo_lane < radius, top_l, pltpu.roll(bot_l, radius, 1))
        send_a[n, :rows] = jnp.where(even_x, to_right, to_left)
        send_b[n, :rows] = jnp.where(even_x, to_left, to_right)
        send_a[n, rows:] = jnp.where(even_x, corner_right, corner_left)
        send_b[n, rows:] = jnp.where(even_x, corner_left, corner_right)


def pack_cols(info, exposures, recv, first, count, radius, after=()):
    nights, frames, rows, cols = exposures.shape
    out = jax.ShapeDtypeStruct((count, rows + frames * radius, LANES), bf16)
    return call(
        functools.partial(pack_cols_kernel, radius=radius, first=first),
        (out, out),
        [SMEM] + [VMEM] * 3,
        (info, exposures, *recv),
        flops=1 << 26,
        after=after,
        name="pack_cols",
    )


STRIDE = 3


def band_shape(rows, size):
    pitch = rows + 2 * GROUP
    count = -(-size // STRIDE)
    ring = -(-(pitch * count + 2 * GROUP) // LANES) * LANES
    return pitch, count, ring


def bands_kernel(psf, out, *, rows):
    _, size, frames, _ = psf.shape
    nights = out.shape[0]
    radius = (size - 1) // 2
    pitch, count, ring = band_shape(rows, size)
    shape = (size, STRIDE * ring)
    b = lax.broadcasted_iota(jnp.int32, shape, 0)
    c = lax.broadcasted_iota(jnp.int32, shape, 1)
    key = c - (b % STRIDE) * ring - pitch * (b // STRIDE) + radius
    key = jnp.where(key >= ring, key - ring, key)
    key = jnp.where(c // ring == b % STRIDE, key, -1)
    total = jnp.zeros((nights * frames, STRIDE * ring), f32)
    for a in range(size):
        taps = jnp.concatenate([psf[n, a] for n in range(nights)], axis=0)
        total = total + jnp.dot(taps, (key == a).astype(bf16), preferred_element_type=f32)
    for e in range(nights * frames):
        for g in range(STRIDE):
            row = total[e : e + 1, ring * g : ring * (g + 1)]
            row = jnp.broadcast_to(row, (rows, ring))
            band = pltpu.roll(row, 0, 1, stride=1, stride_axis=0).astype(bf16)
            out[e // frames, e % frames, rows * g : rows * (g + 1), :] = band


def make_bands(psf_kernels, rows, after):
    nights, frames, size, _ = psf_kernels.shape
    ring = band_shape(rows, size)[2]
    return call(
        functools.partial(bands_kernel, rows=rows),
        (jax.ShapeDtypeStruct((nights, frames, STRIDE * rows, ring), bf16),),
        [VMEM],
        (jnp.swapaxes(psf_kernels, 1, 2),),
        flops=1 << 28,
        name="make_bands",
        limit=24 << 20,
        after=after,
    )


def filter_kernel(
    info, x, ra, rb, ca, cb, bands, out, border, image_0, image_1, windows_0, windows_1,
    *, radius, night, half, start
):
    frames, rows, cols = out.shape
    tiles = cols // LANES
    size = 2 * radius + 1
    pitch, count, ring = band_shape(rows, size)
    packed = ra.shape[1]
    extra = pitch - rows
    even_y = info[0] == 0
    even_x = info[1] == 0
    zero = jnp.zeros((), bf16)
    top_ok = info[2] > 0
    bot_ok = info[2] < info[4] - 1
    left_ok = info[3] > 0
    right_ok = info[3] < info[5] - 1

    col_l = jnp.where(left_ok, jnp.where(even_x, cb[half], ca[half]), zero)
    col_r = jnp.where(right_ok, jnp.where(even_x, ca[half], cb[half]), zero)
    halo_lane = lane_iota((packed, LANES))
    corner_l, corner_r = col_l[rows:], col_r[rows:]
    side_top = jnp.where(
        halo_lane < radius,
        corner_r,
        jnp.where(halo_lane >= LANES - radius, pltpu.roll(corner_l, LANES - radius, 1), zero),
    )
    side_bot = jnp.where(
        halo_lane < radius,
        pltpu.roll(corner_r, LANES - radius, 1),
        jnp.where(halo_lane >= LANES - radius, pltpu.roll(corner_l, LANES - 2 * radius, 1), zero),
    )
    top = jnp.concatenate([jnp.where(even_y, rb[half], ra[half]), side_top], axis=1)
    bot = jnp.concatenate([jnp.where(even_y, ra[half], rb[half]), side_bot], axis=1)
    top = jnp.where(top_ok, top, zero)
    bot = jnp.where(bot_ok, bot, zero)
    top = pltpu.roll(top, cols + LANES - STRIDE, 1)
    shape = (frames * extra, packed)
    r = lax.broadcasted_iota(jnp.int32, shape, 0)
    c = lax.broadcasted_iota(jnp.int32, shape, 1)
    frame, place = r // extra + start, r % extra
    sel_bot = ((place < radius) & (c == frame * radius + place)).astype(bf16)
    from_top = place - (extra - radius)
    sel_top = ((from_top >= 0) & (c == frame * radius + from_top)).astype(bf16)
    border[...] = (
        jnp.dot(sel_bot, bot, preferred_element_type=f32)
        + jnp.dot(sel_top, top, preferred_element_type=f32)
    ).astype(bf16)

    lane = lane_iota((rows, LANES))
    lane_all = lane_iota((pitch, LANES))
    first = pitch * count
    last = ring - extra
    if last > first:
        for windows in (windows_0, windows_1):
            windows[first:last, :] = jnp.zeros((last - first, cols + LANES), bf16)

    def turn(shift, source, mask_lane):
        if shift == 0:
            return source
        turned = [pltpu.roll(t, shift % LANES, 1) for t in source]
        size = len(source)
        if shift > 0:
            return [jnp.where(mask_lane < shift, turned[k - 1], turned[k]) for k in range(size)]
        return [
            jnp.where(mask_lane < LANES + shift, turned[k], turned[(k + 1) % size])
            for k in range(size)
        ]

    middle = (STRIDE - 1) // 2

    def prepare(e, image, windows):
        image[:rows, :cols] = x[night, start + e]
        side_r = pltpu.roll(col_r[:rows], (LANES - radius * (start + e)) % LANES, 1)
        side_l = pltpu.roll(col_l[:rows], (2 * LANES - radius - radius * (start + e)) % LANES, 1)
        image[:rows, cols:] = jnp.where(
            lane < radius, side_r, jnp.where(lane >= LANES - radius, side_l, zero)
        )
        image[rows:] = border[pl.ds(pl.multiple_of(e * extra, extra), extra)]
        parts = [image[:, LANES * k : LANES * (k + 1)] for k in range(tiles + 1)]
        for w in range(count):
            shift = radius - middle - STRIDE * w
            for k, value in enumerate(turn(shift, parts, lane_all)):
                windows[pitch * w : pitch * (w + 1), LANES * k : LANES * (k + 1)] = value
        tail = [t[rows:] for t in parts]
        for k, value in enumerate(turn(radius - middle + STRIDE, tail, lane_all[:extra])):
            windows[last:, LANES * k : LANES * (k + 1)] = value

    def combine(e, windows):
        sums = jnp.dot(bands[night, start + e], windows[...], preferred_element_type=f32)
        total = None
        for g in range(STRIDE):
            part = sums[rows * g : rows * (g + 1)]
            part = [part[:, LANES * k : LANES * (k + 1)] for k in range(tiles + 1)]
            part = turn(middle - g, part, lane)
            total = part if total is None else [a + b for a, b in zip(total, part)]
        for k in range(tiles):
            out[e, :, LANES * k : LANES * (k + 1)] = total[k]

    def pair(i, carry):
        prepare(2 * i + 1, image_1, windows_1)
        combine(2 * i, windows_0)
        prepare(jnp.minimum(2 * i + 2, frames - 1), image_0, windows_0)
        combine(2 * i + 1, windows_1)
        return carry

    prepare(0, image_0, windows_0)
    lax.fori_loop(0, frames // 2, pair, 0)
    if frames % 2:
        combine(frames - 1, windows_0)


def filter_night(
    info, exposures, night, half, bands, got_rows, got_cols, start, count, radius, after
):
    nights, frames, rows, cols = exposures.shape
    pitch, _, ring = band_shape(rows, 2 * radius + 1)
    return call(
        functools.partial(filter_kernel, radius=radius, night=night, half=half, start=start),
        (jax.ShapeDtypeStruct((count, rows, cols), f32),),
        [SMEM] + [VMEM] * 6,
        (info, exposures, *got_rows, *got_cols, bands),
        scratch=[
            pltpu.VMEM((count * 2 * GROUP, cols + LANES), bf16),
            pltpu.VMEM((pitch, cols + LANES), bf16),
            pltpu.VMEM((pitch, cols + LANES), bf16),
            pltpu.VMEM((ring, cols + LANES), bf16),
            pltpu.VMEM((ring, cols + LANES), bf16),
        ],
        after=after,
        flops=2 * count * STRIDE * rows * ring * cols,
        name="filter_night",
    )


QUAD = 4
UNITS = 4
BLOCKS = 2
FIELDS = 2 * QUAD
DOWN, UP = (0, 1, 4, 5), (2, 3, 6, 7)
RIGHT, LEFT = (0, 2, 4, 6), (1, 3, 5, 7)


def plane_of(group, q, planes):
    return (q // 2) * (planes // 2) + 2 * group + q % 2


def strip_shape(length, width):
    return jax.ShapeDtypeStruct((len(DOWN) * length + GROUP, width), jnp.int16)


def put_sides(odd, source, first_way, second_way, axis, margin, sends):
    size = source.shape[axis]
    end = pl.multiple_of((size - margin) * (1 - odd), SUB if axis == 1 else LANES)
    begin = pl.multiple_of((size - margin) * odd, SUB if axis == 1 else LANES)
    for send, start, swapped in ((sends[0], end, odd), (sends[1], begin, 1 - odd)):
        cut = pl.ds(start, margin)

        def piece(a, b, cut=cut, swapped=swapped):
            f = a + (b - a) * swapped
            return lambda: source[f, cut, :] if axis == 1 else source[f, :, cut]

        put_codes(send, [piece(a, b) for a, b in zip(first_way, second_way)])


def move_rows_kernel(
    info, offsets, field, ra, rb, out, send_a, send_b, *above, margin, side, night, planes
):
    group_planes, group = planes
    fields, rows, cols = field.shape
    even = info[0] == 0
    top_ok = jnp.where(info[2] > 0, 1.0, 0.0)
    bot_ok = jnp.where(info[2] < info[4] - 1, 1.0, 0.0)
    sub = lax.broadcasted_iota(jnp.int32, (SUB, LANES), 0)

    def turn(source, start, result):
        base = (start // SUB) * SUB
        rest = start % SUB
        back = (SUB - rest) % SUB
        keep = sub < SUB - rest
        for k in range(cols // LANES):
            lanes = slice(LANES * k, LANES * (k + 1))
            turned = None
            for j in range(rows // SUB + 1):
                before = turned
                at = pl.ds(pl.multiple_of(base + SUB * j, SUB), SUB)
                turned = pltpu.roll(source[at, lanes], back, 0)
                if j:
                    result[SUB * (j - 1) : SUB * j, lanes] = jnp.where(keep, before, turned)

    from_above = get_codes(even, rb, ra, len(DOWN), top_ok)
    from_below = get_codes(even, ra, rb, len(UP), bot_ok)
    for j in range(len(DOWN)):
        for f, got in ((DOWN[j], from_above), (UP[j], from_below)):
            source = above[f]
            offset = offsets[night, 0, plane_of(group, f % QUAD, group_planes)]
            if f in DOWN:
                source[:margin] = got(j)
                source[margin : margin + rows] = field[f]
                start = margin - offset
            else:
                source[:rows] = field[f]
                source[rows : rows + margin] = got(j)
                start = -offset
            source[rows + margin :] = jnp.zeros((SUB, cols), f32)
            turn(source, start, out.at[f])
    put_sides(info[1], out, RIGHT, LEFT, 2, side, (send_a, send_b))


def move_rows(info, offsets, field, recv, night, planes, after):
    fields, rows, cols = field.shape
    margin = 3 * rows // 4
    side = 3 * cols // 4
    strip = strip_shape(rows, side)
    return call(
        functools.partial(
            move_rows_kernel, margin=margin, side=side, night=night, planes=planes
        ),
        (jax.ShapeDtypeStruct(field.shape, f32), strip, strip),
        [SMEM, SMEM, VMEM, VMEM, VMEM],
        (info, offsets, field, *recv),
        scratch=[pltpu.VMEM((rows + margin + SUB, cols), f32)] * fields,
        flops=1 << 27,
        after=after,
        name="move_rows",
    )


def move_columns(info, offsets, night, field, ca, cb, out, wide, side, planes):
    group_planes, group = planes
    fields, rows, cols = field.shape
    even = info[1] == 0
    left_ok = jnp.where(info[3] > 0, 1.0, 0.0)
    right_ok = jnp.where(info[3] < info[5] - 1, 1.0, 0.0)
    lane = lane_iota((SUB, LANES))

    def turn(source, start, result):
        base = (start // LANES) * LANES
        rest = start % LANES
        back = (LANES - rest) % LANES
        keep = lane < LANES - rest
        for k in range(rows // SUB):
            at = slice(SUB * k, SUB * (k + 1))
            turned = None
            for j in range(cols // LANES + 1):
                before = turned
                lanes = pl.ds(pl.multiple_of(base + LANES * j, LANES), LANES)
                turned = pltpu.roll(source[at, lanes], back, 1)
                if j:
                    result[at, LANES * (j - 1) : LANES * j] = jnp.where(keep, before, turned)

    from_left = get_codes(even, cb, ca, len(RIGHT), left_ok)
    from_right = get_codes(even, ca, cb, len(LEFT), right_ok)
    for j in range(len(RIGHT)):
        for f, got in ((RIGHT[j], from_left), (LEFT[j], from_right)):
            source = wide[f]
            offset = offsets[night, 1, plane_of(group, f % QUAD, group_planes)]
            if f in RIGHT:
                source[:, :side] = got(j)
                source[:, side : side + cols] = field[f]
                start = side - offset
            else:
                source[:, :cols] = field[f]
                source[:, cols : cols + side] = got(j)
                start = -offset
            source[:, cols + side :] = jnp.zeros((rows, LANES), f32)
            turn(source, start, out.at[f])


def stack_kernel(*refs, night, last, margin, side, planes, parts, spare):
    info, offsets, weights, masks, *refs = refs
    images, refs = refs[:parts], refs[parts:]
    filtered = [part.at[e] for part in images for e in range(part.shape[0])]
    moved = night > 0
    group_planes, group = planes
    if moved:
        field, ca, cb, *refs = refs
        _, rows, cols = field.shape
    else:
        start_flux, start_weight, *refs = refs
        rows, cols = start_flux.shape[1:]
    refs = refs[spare:]
    if last:
        out_flux, out_weight, *refs = refs
    else:
        out, send_a, send_b, *refs = refs
    table = refs[0]
    frames = len(filtered)
    tiles = cols // LANES
    lead = 2 if moved else 0

    def prepare():
        if moved:
            move_columns(
                info, offsets, night - 1, field, ca, cb, refs[1], refs[2:], side, planes
            )
        grown = None
        for e in range(frames):
            gain = weights[night, e]
            if e >= lead:
                grown = gain if grown is None else grown + gain
            filled = jnp.full((SUB, LANES), gain, f32)
            band = band_scale / jnp.sqrt(filled)
            table[0, e] = filled
            table[1, e] = band
            table[2, e] = -band
            table[3, e] = jnp.full((SUB, LANES), 0.0 if grown is None else grown, f32)

    ids = [plane_of(group, q, group_planes) for q in range(QUAD)]

    def chunk(first, c, first_out):
        cells = [(u, q) for u in range(UNITS) for q in range(QUAD)]
        rows_of = [pl.ds(pl.multiple_of(first + SUB * u, SUB), SUB) for u in range(UNITS)]
        outs_of = [pl.ds(pl.multiple_of(first_out + SUB * u, SUB), SUB) for u in range(UNITS)]
        mean, after, f, held = {}, {}, {}, {}
        for u, q in cells:
            if moved:
                f[u, q] = refs[1][q, rows_of[u], c]
                held[u, q] = refs[1][QUAD + q, rows_of[u], c]
            else:
                f[u, q] = start_flux[ids[q], rows_of[u], c]
                held[u, q] = start_weight[ids[q], rows_of[u], c]
        for e in range(frames):
            value = [filtered[e][r, c] for r in rows_of]
            mask = [masks[night, e, r, c] for r in rows_of]
            gain, above, below, grown = (table[k, e] for k in range(4))
            for k in cells:
                u, q = k
                if e == lead:
                    after[k] = held[k] + table[3, frames - 1]
                    held[k] = jnp.maximum(held[k], weight_floor)
                    mean[k] = f[k] * pltpu.reciprocal(held[k], approx=True)
                if e < lead:
                    total = jnp.maximum(held[k], weight_floor)
                    mean[k] = f[k] * pltpu.reciprocal(total, approx=True)
                step = value[u] - mean[k]
                clipped = jnp.minimum(jnp.maximum(step, below), above)
                step = jnp.where((mask[u] & (1 << ids[q])) != 0, clipped, step)
                if e < lead:
                    f[k] = f[k] + gain * (mean[k] + step)
                    held[k] = held[k] + gain
                else:
                    part = gain * pltpu.reciprocal(held[k] + grown, approx=True)
                    mean[k] = mean[k] + part * step
        grown = table[3, frames - 1]
        for k in cells:
            u, q = k
            flux = mean[k] * (held[k] + grown)
            if last:
                out_flux[q // 2, 0, q % 2, outs_of[u], c] = flux
                out_weight[q // 2, 0, q % 2, outs_of[u], c] = after[k]
            else:
                out[q, outs_of[u], c] = flux
                out[QUAD + q, outs_of[u], c] = after[k]

    step_rows = SUB * UNITS

    def lanes(k):
        return pl.ds(pl.multiple_of(k * LANES, LANES), LANES)

    if last:
        i = pl.program_id(0)
        block = out_flux.shape[3]
        pl.when(i == 0)(prepare)

        @pl.loop(0, block // step_rows * tiles)
        def _(k):
            row = k // tiles * step_rows
            chunk(i * block + row, lanes(k % tiles), row)
    else:
        prepare()

        @pl.loop(0, rows // step_rows * tiles)
        def _(k):
            row = k // tiles * step_rows
            chunk(row, lanes(k % tiles), row)

        put_sides(info[0], out, DOWN, UP, 1, margin, (send_a, send_b))


def stack_night(info, offsets, weights, masks, images, state, night, planes, earlier, after):
    nights, frames, rows, cols = masks.shape
    margin = 3 * rows // 4
    side = 3 * cols // 4
    last = night == nights - 1
    scratch = [pltpu.VMEM((4, frames, SUB, LANES), f32)]
    if night > 0:
        scratch.append(pltpu.VMEM((FIELDS, rows, cols), f32))
        scratch += [pltpu.VMEM((rows, cols + side + LANES), f32)] * FIELDS
    args = (info, offsets, weights, masks, *images, *state)
    specs = [SMEM] * 3 + [VMEM] * (len(args) - 3)
    kernel = functools.partial(
        stack_kernel, night=night, last=last, margin=margin, side=side, planes=planes,
        parts=len(images), spare=len(earlier),
    )
    known = dict(
        scratch=scratch,
        flops=12 * frames * QUAD * rows * cols,
        name="stack_night",
        after=after,
    )
    if not last:
        strip = strip_shape(margin, cols)
        out = jax.ShapeDtypeStruct((FIELDS, rows, cols), f32)
        return call(kernel, (out, strip, strip), specs, args, **known)
    total, group = planes
    out = jax.ShapeDtypeStruct((2, total // QUAD, 2, rows, cols), f32)
    block = pl.BlockSpec((2, 1, 2, rows // BLOCKS, cols), lambda i: (0, group, 0, i, 0))
    return call(
        kernel,
        (out, out),
        specs + [pl.BlockSpec(memory_space=pl.ANY)] * len(earlier),
        (*args, *earlier),
        grid=(BLOCKS,),
        out_specs=(block, block),
        aliases={len(args) + i: i for i in range(len(earlier))},
        **known,
    )


def per_device(
    exposures, psf_kernels, clip_masks, exposure_weights, plane_offsets, start_flux, start_weight
):
    nights, frames, rows, cols = exposures.shape
    planes_total = start_flux.shape[0]
    radius = (psf_kernels.shape[2] - 1) // 2
    iy, ix = lax.axis_index("sy"), lax.axis_index("sx")
    ny, nx = lax.axis_size("sy"), lax.axis_size("sx")
    info = jnp.stack([iy % 2, ix % 2, iy, ix, jnp.int32(ny), jnp.int32(nx)]).astype(jnp.int32)

    offsets = jnp.swapaxes(plane_offsets, 1, 2)

    *sent, done = pack_rows(info, exposures, 0, 1, radius)
    rows_first = swap_rows(sent)
    bands, done = make_bands(psf_kernels, rows, (done,))
    *sent, done = pack_cols(info, exposures, rows_first, 0, 1, radius, (done,))
    cols_first = swap_columns(sent)
    *sent, done = pack_rows(info, exposures, 1, nights - 1, radius, (done,))
    rows_later = swap_rows(sent)
    image, done = filter_night(
        info, exposures, 0, 0, bands, rows_first, cols_first, 0, frames, radius, (done,)
    )

    groups = [(planes_total, g) for g in range(planes_total // QUAD)]
    states = [(start_flux, start_weight)] * len(groups)
    results = ()
    for n in range(nights):
        fields = []
        sent = []
        for group, state in zip(groups, states):
            first, *strips, done = stack_night(
                info, offsets, exposure_weights, clip_masks, (image,), state, n, group, results,
                (done,),
            )
            fields.append(first)
            if n == nights - 1:
                results = (first, *strips)
            else:
                sent.append(swap_rows(strips))
        if n == nights - 1:
            shape = (planes_total, rows, cols)
            return tuple(r.reshape(shape) for r in results)
        if n == 0:
            *later, done = pack_cols(info, exposures, rows_later, 1, nights - 1, radius, (done,))
            cols_later = swap_columns(later)
        states = []
        for i, group in enumerate(groups):
            field, *strips, done = move_rows(
                info, offsets, fields[i], sent[i], n, group, (done,)
            )
            states.append((field, *swap_columns(strips)))
            if i == 0:
                image, done = filter_night(
                    info, exposures, n + 1, n, bands, rows_later, cols_later, 0, frames, radius,
                    (done,),
                )


def solution(mesh):
    return jax.shard_map(
        per_device,
        mesh=mesh,
        in_specs=(
            P(None, None, "sy", "sx"),
            P(),
            P(None, None, "sy", "sx"),
            P(),
            P(),
            P(None, "sy", "sx"),
            P(None, "sy", "sx"),
        ),
        out_specs=(P(None, "sy", "sx"), P(None, "sy", "sx")),
        check_vma=False,
    )
```

```python
import functools
import math

import jax
import jax.numpy as jnp
from jax import lax
from jax.experimental import pallas as pl
from jax.experimental.pallas import tpu as pltpu
from jax.sharding import PartitionSpec as P

band_scale = 1.5
weight_floor = 1.0
LANES = 128
SUB = 8
GROUP = 16
bf16 = jnp.bfloat16
f32 = jnp.float32
SMEM = pl.BlockSpec(memory_space=pltpu.SMEM)
VMEM = pl.BlockSpec(memory_space=pltpu.VMEM)


def call(
    kernel, outs, in_specs, args, *, name, flops, scratch=(), limit=16 << 20, after=(),
    grid=(), out_specs=None, aliases=None,
):
    size = sum(math.prod(o.shape) * o.dtype.itemsize for o in outs)
    known = len(args)
    begin = known + len(after)
    end = begin + len(outs)
    token = jax.ShapeDtypeStruct((SUB, LANES), f32)

    def ordered(*refs):
        refs[end][...] = jnp.zeros((SUB, LANES), f32)
        kernel(*refs[:known], *refs[begin:end], *refs[end + 1 :])

    return pl.pallas_call(
        ordered,
        grid=grid,
        out_shape=(*outs, token),
        in_specs=list(in_specs) + [VMEM] * len(after),
        out_specs=(VMEM,) * (len(outs) + 1) if out_specs is None else (*out_specs, VMEM),
        scratch_shapes=list(scratch),
        input_output_aliases=aliases or {},
        compiler_params=pltpu.CompilerParams(vmem_limit_bytes=limit),
        cost_estimate=pl.CostEstimate(flops=flops, bytes_accessed=2 * size, transcendentals=0),
        name=name,
    )(*args, *after)


def swap_pairs(axis, parity):
    ny, nx = lax.axis_size("sy"), lax.axis_size("sx")
    count, others = (ny, nx) if axis == "sy" else (nx, ny)
    pairs = []
    for j in range(others):
        for i in range(count):
            k = i + 1 if (i - parity) % 2 == 0 else i - 1
            if axis == "sx":
                k %= count
            target = (k, j) if 0 <= k < count else (i, j ^ 1)
            if axis == "sy":
                pairs.append((i * nx + j, target[0] * nx + target[1]))
            else:
                pairs.append((j * nx + i, target[1] * nx + target[0]))
    return pairs


def swap(value, axis, parity):
    return lax.ppermute(value, ("sy", "sx"), swap_pairs(axis, parity))


def swap_rows(values):
    return [swap(v, "sy", parity) for parity, v in enumerate(values)]


def swap_columns(values):
    return [swap(v, "sx", parity) for parity, v in enumerate(values)]


CODES = 32767.0
STEPS = 8.0


def put_codes(send, pieces):
    length, width = pieces[0]().shape
    row = lax.broadcasted_iota(jnp.int32, (GROUP, width), 0)
    scales = jnp.zeros((GROUP, width), f32)
    for j, piece in enumerate(pieces):
        v = piece()
        top = jnp.max(jnp.max(jnp.abs(v), axis=0, keepdims=True), axis=1, keepdims=True)
        power = jnp.ceil(jnp.log2(jnp.maximum(top, 1e-12)) * STEPS) + 1.0
        t = v * (jnp.exp2(power * (-1.0 / STEPS)) * (CODES * CODES))
        code = t * lax.rsqrt(jnp.abs(t) + 1e-30)
        send[length * j : length * (j + 1), :] = to_int16(code)
        scales = jnp.where(row == j, power, scales)
    send[length * len(pieces) :, :] = to_int16(scales)


def to_int16(v):
    return v.astype(jnp.int32).astype(jnp.int16)


def get_codes(use_first, first, second, count, keep):
    length = (first.shape[0] - GROUP) // count

    def rows(start, size):
        both = jnp.where(use_first, first[start : start + size, :], second[start : start + size, :])
        return both.astype(jnp.int32).astype(f32)

    scale = jnp.exp2(rows(length * count, GROUP) * (1.0 / STEPS)) * (keep / (CODES * CODES))

    def piece(j):
        code = rows(length * j, length)
        return code * (jnp.abs(code) + 1.0) * scale[j : j + 1, :]

    return piece


def lane_iota(shape):
    return lax.broadcasted_iota(jnp.int32, shape, len(shape) - 1)


def pack_cols_kernel(info, x, send_a, send_b, *, radius):
    nights, frames, rows, cols = x.shape
    even_x = info[1] == 0
    lane = lane_iota((rows, LANES))
    for n in range(nights):
        to_right = jnp.zeros((rows, LANES), bf16)
        to_left = jnp.zeros((rows, LANES), bf16)
        for e in range(frames):
            here = (lane >= radius * e) & (lane < radius * (e + 1))
            shift = (radius * (e + 1)) % LANES
            right = x[n, e, :, cols - LANES :]
            to_right = jnp.where(here, pltpu.roll(right, shift, 1), to_right)
            to_left = jnp.where(here, pltpu.roll(x[n, e, :, :LANES], radius * e, 1), to_left)
        send_a[n] = jnp.where(even_x, to_right, to_left)
        send_b[n] = jnp.where(even_x, to_left, to_right)


def pack_cols(info, exposures, radius):
    nights, frames, rows, cols = exposures.shape
    out = jax.ShapeDtypeStruct((nights, rows, LANES), bf16)
    return call(
        functools.partial(pack_cols_kernel, radius=radius),
        (out, out),
        [SMEM, VMEM],
        (info, exposures),
        flops=1 << 26,
        name="pack_cols",
    )


def received_cols(info, ca, cb, night):
    even_x = info[1] == 0
    zero = jnp.zeros((), bf16)
    left = jnp.where(info[3] > 0, jnp.where(even_x, cb[night], ca[night]), zero)
    right = jnp.where(info[3] < info[5] - 1, jnp.where(even_x, ca[night], cb[night]), zero)
    return left, right


def side_tile(left, right, e, radius):
    lane = lane_iota(left.shape)
    zero = jnp.zeros((), bf16)
    right = pltpu.roll(right, (LANES - radius * e) % LANES, 1)
    left = pltpu.roll(left, (2 * LANES - radius - radius * e) % LANES, 1)
    return jnp.where(lane < radius, right, jnp.where(lane >= LANES - radius, left, zero))


def pack_rows_kernel(info, x, ca, cb, send_a, send_b, *, radius, first):
    frames, tile_rows, cols = x.shape[1:]
    rows = frames * radius
    even = info[0] == 0
    shape = (rows, frames * GROUP)
    r = lax.broadcasted_iota(jnp.int32, shape, 0)
    c = lax.broadcasted_iota(jnp.int32, shape, 1)
    base = (r // radius) * GROUP + r % radius
    sel_top = (c == base).astype(bf16)
    sel_bot = (c == base + (GROUP - radius)).astype(bf16)
    for n in range(send_a.shape[0]):
        left, right = received_cols(info, ca, cb, first + n)

        def strip(sel, start):
            at = slice(start, start + GROUP)
            ends = [side_tile(left[at], right[at], e, radius) for e in range(frames)]
            block = x[first + n, :, at, :].reshape(frames * GROUP, cols)
            block = jnp.concatenate([block, jnp.concatenate(ends, axis=0)], axis=1)
            return jnp.dot(sel, block, preferred_element_type=f32).astype(bf16)

        up = strip(sel_top, 0)
        down = strip(sel_bot, tile_rows - GROUP)
        send_a[n] = jnp.where(even, down, up)
        send_b[n] = jnp.where(even, up, down)


def pack_rows(info, exposures, got_cols, first, count, radius, after):
    nights, frames, rows, cols = exposures.shape
    out = jax.ShapeDtypeStruct((count, frames * radius, cols + LANES), bf16)
    return call(
        functools.partial(pack_rows_kernel, radius=radius, first=first),
        (out, out),
        [SMEM] + [VMEM] * 3,
        (info, exposures, *got_cols),
        flops=1 << 26,
        name="pack_rows",
        after=after,
    )


STRIDE = 3


def band_shape(rows, size):
    pitch = rows + 2 * GROUP
    count = -(-size // STRIDE)
    ring = -(-(pitch * count + 2 * GROUP) // LANES) * LANES
    return pitch, count, ring


def bands_kernel(psf, out, *, rows):
    _, size, frames, _ = psf.shape
    nights = out.shape[0]
    radius = (size - 1) // 2
    pitch, count, ring = band_shape(rows, size)
    shape = (size, STRIDE * ring)
    b = lax.broadcasted_iota(jnp.int32, shape, 0)
    c = lax.broadcasted_iota(jnp.int32, shape, 1)
    key = c - (b % STRIDE) * ring - pitch * (b // STRIDE) + radius
    key = jnp.where(key >= ring, key - ring, key)
    key = jnp.where(c // ring == b % STRIDE, key, -1)
    total = jnp.zeros((nights * frames, STRIDE * ring), f32)
    for a in range(size):
        taps = jnp.concatenate([psf[n, a] for n in range(nights)], axis=0)
        total = total + jnp.dot(taps, (key == a).astype(bf16), preferred_element_type=f32)
    for e in range(nights * frames):
        for g in range(STRIDE):
            row = total[e : e + 1, ring * g : ring * (g + 1)]
            row = jnp.broadcast_to(row, (rows, ring))
            band = pltpu.roll(row, 0, 1, stride=1, stride_axis=0).astype(bf16)
            out[e // frames, e % frames, rows * g : rows * (g + 1), :] = band


def make_bands(psf_kernels, rows, after):
    nights, frames, size, _ = psf_kernels.shape
    ring = band_shape(rows, size)[2]
    return call(
        functools.partial(bands_kernel, rows=rows),
        (jax.ShapeDtypeStruct((nights, frames, STRIDE * rows, ring), bf16),),
        [VMEM],
        (jnp.swapaxes(psf_kernels, 1, 2),),
        flops=1 << 28,
        name="make_bands",
        limit=24 << 20,
        after=after,
    )


def filter_kernel(
    info, x, ra, rb, ca, cb, bands, out, border, image_0, image_1, windows_0, windows_1,
    *, radius, night, half, start
):
    frames, rows, cols = out.shape
    tiles = cols // LANES
    size = 2 * radius + 1
    pitch, count, ring = band_shape(rows, size)
    packed = ra.shape[1]
    extra = pitch - rows
    even_y = info[0] == 0
    zero = jnp.zeros((), bf16)
    top_ok = info[2] > 0
    bot_ok = info[2] < info[4] - 1
    col_l, col_r = received_cols(info, ca, cb, night)
    top = jnp.where(even_y, rb[half], ra[half])
    bot = jnp.where(even_y, ra[half], rb[half])
    top = jnp.where(top_ok, top, zero)
    bot = jnp.where(bot_ok, bot, zero)
    top = pltpu.roll(top, cols + LANES - STRIDE, 1)
    shape = (frames * extra, packed)
    r = lax.broadcasted_iota(jnp.int32, shape, 0)
    c = lax.broadcasted_iota(jnp.int32, shape, 1)
    frame, place = r // extra + start, r % extra
    sel_bot = ((place < radius) & (c == frame * radius + place)).astype(bf16)
    from_top = place - (extra - radius)
    sel_top = ((from_top >= 0) & (c == frame * radius + from_top)).astype(bf16)
    border[...] = (
        jnp.dot(sel_bot, bot, preferred_element_type=f32)
        + jnp.dot(sel_top, top, preferred_element_type=f32)
    ).astype(bf16)

    lane = lane_iota((rows, LANES))
    lane_all = lane_iota((pitch, LANES))
    first = pitch * count
    last = ring - extra
    if last > first:
        for windows in (windows_0, windows_1):
            windows[first:last, :] = jnp.zeros((last - first, cols + LANES), bf16)

    def turn(shift, source, mask_lane):
        if shift == 0:
            return source
        turned = [pltpu.roll(t, shift % LANES, 1) for t in source]
        size = len(source)
        if shift > 0:
            return [jnp.where(mask_lane < shift, turned[k - 1], turned[k]) for k in range(size)]
        return [
            jnp.where(mask_lane < LANES + shift, turned[k], turned[(k + 1) % size])
            for k in range(size)
        ]

    middle = (STRIDE - 1) // 2

    def prepare(e, image, windows):
        image[:rows, :cols] = x[night, start + e]
        image[:rows, cols:] = side_tile(col_l, col_r, start + e, radius)
        image[rows:] = border[pl.ds(pl.multiple_of(e * extra, extra), extra)]
        parts = [image[:, LANES * k : LANES * (k + 1)] for k in range(tiles + 1)]
        for w in range(count):
            shift = radius - middle - STRIDE * w
            for k, value in enumerate(turn(shift, parts, lane_all)):
                windows[pitch * w : pitch * (w + 1), LANES * k : LANES * (k + 1)] = value
        tail = [t[rows:] for t in parts]
        for k, value in enumerate(turn(radius - middle + STRIDE, tail, lane_all[:extra])):
            windows[last:, LANES * k : LANES * (k + 1)] = value

    def combine(e, windows):
        sums = jnp.dot(bands[night, start + e], windows[...], preferred_element_type=f32)
        total = None
        for g in range(STRIDE):
            part = sums[rows * g : rows * (g + 1)]
            part = [part[:, LANES * k : LANES * (k + 1)] for k in range(tiles + 1)]
            part = turn(middle - g, part, lane)
            total = part if total is None else [a + b for a, b in zip(total, part)]
        for k in range(tiles):
            out[e, :, LANES * k : LANES * (k + 1)] = total[k]

    def pair(i, carry):
        prepare(2 * i + 1, image_1, windows_1)
        combine(2 * i, windows_0)
        prepare(jnp.minimum(2 * i + 2, frames - 1), image_0, windows_0)
        combine(2 * i + 1, windows_1)
        return carry

    prepare(0, image_0, windows_0)
    lax.fori_loop(0, frames // 2, pair, 0)
    if frames % 2:
        combine(frames - 1, windows_0)


def filter_night(
    info, exposures, night, half, bands, got_rows, got_cols, start, count, radius, after
):
    nights, frames, rows, cols = exposures.shape
    pitch, _, ring = band_shape(rows, 2 * radius + 1)
    return call(
        functools.partial(filter_kernel, radius=radius, night=night, half=half, start=start),
        (jax.ShapeDtypeStruct((count, rows, cols), f32),),
        [SMEM] + [VMEM] * 6,
        (info, exposures, *got_rows, *got_cols, bands),
        scratch=[
            pltpu.VMEM((count * 2 * GROUP, cols + LANES), bf16),
            pltpu.VMEM((pitch, cols + LANES), bf16),
            pltpu.VMEM((pitch, cols + LANES), bf16),
            pltpu.VMEM((ring, cols + LANES), bf16),
            pltpu.VMEM((ring, cols + LANES), bf16),
        ],
        after=after,
        flops=2 * count * STRIDE * rows * ring * cols,
        name="filter_night",
    )


QUAD = 4
UNITS = 4
BLOCKS = 2
FIELDS = 2 * QUAD
DOWN, UP = (0, 1, 4, 5), (2, 3, 6, 7)
RIGHT, LEFT = (0, 2, 4, 6), (1, 3, 5, 7)


def plane_of(group, q, planes):
    return (q // 2) * (planes // 2) + 2 * group + q % 2


def strip_shape(length, width):
    return jax.ShapeDtypeStruct((len(DOWN) * length + GROUP, width), jnp.int16)


def put_sides(odd, source, first_way, second_way, axis, margin, sends):
    size = source.shape[axis]
    end = pl.multiple_of((size - margin) * (1 - odd), SUB if axis == 1 else LANES)
    begin = pl.multiple_of((size - margin) * odd, SUB if axis == 1 else LANES)
    for send, start, swapped in ((sends[0], end, odd), (sends[1], begin, 1 - odd)):
        cut = pl.ds(start, margin)

        def piece(a, b, cut=cut, swapped=swapped):
            f = a + (b - a) * swapped
            return lambda: source[f, cut, :] if axis == 1 else source[f, :, cut]

        put_codes(send, [piece(a, b) for a, b in zip(first_way, second_way)])


def move_rows_kernel(
    info, offsets, field, ra, rb, out, send_a, send_b, *above, margin, side, night, planes
):
    group_planes, group = planes
    fields, rows, cols = field.shape
    even = info[0] == 0
    top_ok = jnp.where(info[2] > 0, 1.0, 0.0)
    bot_ok = jnp.where(info[2] < info[4] - 1, 1.0, 0.0)
    sub = lax.broadcasted_iota(jnp.int32, (SUB, LANES), 0)

    def turn(source, start, result):
        base = (start // SUB) * SUB
        rest = start % SUB
        back = (SUB - rest) % SUB
        keep = sub < SUB - rest
        for k in range(cols // LANES):
            lanes = slice(LANES * k, LANES * (k + 1))
            turned = None
            for j in range(rows // SUB + 1):
                before = turned
                at = pl.ds(pl.multiple_of(base + SUB * j, SUB), SUB)
                turned = pltpu.roll(source[at, lanes], back, 0)
                if j:
                    result[SUB * (j - 1) : SUB * j, lanes] = jnp.where(keep, before, turned)

    from_above = get_codes(even, rb, ra, len(DOWN), top_ok)
    from_below = get_codes(even, ra, rb, len(UP), bot_ok)
    for j in range(len(DOWN)):
        for f, got in ((DOWN[j], from_above), (UP[j], from_below)):
            source = above[f]
            offset = offsets[night, 0, plane_of(group, f % QUAD, group_planes)]
            if f in DOWN:
                source[:margin] = got(j)
                source[margin : margin + rows] = field[f]
                start = margin - offset
            else:
                source[:rows] = field[f]
                source[rows : rows + margin] = got(j)
                start = -offset
            source[rows + margin :] = jnp.zeros((SUB, cols), f32)
            turn(source, start, out.at[f])
    put_sides(info[1], out, RIGHT, LEFT, 2, side, (send_a, send_b))


def move_rows(info, offsets, field, recv, night, planes, after):
    fields, rows, cols = field.shape
    margin = 3 * rows // 4
    side = 3 * cols // 4
    strip = strip_shape(rows, side)
    return call(
        functools.partial(
            move_rows_kernel, margin=margin, side=side, night=night, planes=planes
        ),
        (jax.ShapeDtypeStruct(field.shape, f32), strip, strip),
        [SMEM, SMEM, VMEM, VMEM, VMEM],
        (info, offsets, field, *recv),
        scratch=[pltpu.VMEM((rows + margin + SUB, cols), f32)] * fields,
        flops=1 << 27,
        after=after,
        name="move_rows",
    )


def move_columns(info, offsets, night, field, ca, cb, out, wide, side, planes):
    group_planes, group = planes
    fields, rows, cols = field.shape
    even = info[1] == 0
    left_ok = jnp.where(info[3] > 0, 1.0, 0.0)
    right_ok = jnp.where(info[3] < info[5] - 1, 1.0, 0.0)
    lane = lane_iota((SUB, LANES))

    def turn(source, start, result):
        base = (start // LANES) * LANES
        rest = start % LANES
        back = (LANES - rest) % LANES
        keep = lane < LANES - rest
        for k in range(rows // SUB):
            at = slice(SUB * k, SUB * (k + 1))
            turned = None
            for j in range(cols // LANES + 1):
                before = turned
                lanes = pl.ds(pl.multiple_of(base + LANES * j, LANES), LANES)
                turned = pltpu.roll(source[at, lanes], back, 1)
                if j:
                    result[at, LANES * (j - 1) : LANES * j] = jnp.where(keep, before, turned)

    from_left = get_codes(even, cb, ca, len(RIGHT), left_ok)
    from_right = get_codes(even, ca, cb, len(LEFT), right_ok)
    for j in range(len(RIGHT)):
        for f, got in ((RIGHT[j], from_left), (LEFT[j], from_right)):
            source = wide[f]
            offset = offsets[night, 1, plane_of(group, f % QUAD, group_planes)]
            if f in RIGHT:
                source[:, :side] = got(j)
                source[:, side : side + cols] = field[f]
                start = side - offset
            else:
                source[:, :cols] = field[f]
                source[:, cols : cols + side] = got(j)
                start = -offset
            source[:, cols + side :] = jnp.zeros((rows, LANES), f32)
            turn(source, start, out.at[f])


def stack_kernel(*refs, night, last, margin, side, planes, parts, spare):
    info, offsets, weights, masks, *refs = refs
    images, refs = refs[:parts], refs[parts:]
    filtered = [part.at[e] for part in images for e in range(part.shape[0])]
    moved = night > 0
    group_planes, group = planes
    if moved:
        field, ca, cb, *refs = refs
        _, rows, cols = field.shape
    else:
        start_flux, start_weight, *refs = refs
        rows, cols = start_flux.shape[1:]
    refs = refs[spare:]
    if last:
        out_flux, out_weight, *refs = refs
    else:
        out, send_a, send_b, *refs = refs
    table = refs[0]
    frames = len(filtered)
    tiles = cols // LANES
    lead = 2 if moved else 0

    def prepare():
        if moved:
            move_columns(
                info, offsets, night - 1, field, ca, cb, refs[1], refs[2:], side, planes
            )
        grown = None
        for e in range(frames):
            gain = weights[night, e]
            if e >= lead:
                grown = gain if grown is None else grown + gain
            filled = jnp.full((SUB, LANES), gain, f32)
            band = band_scale / jnp.sqrt(filled)
            table[0, e] = filled
            table[1, e] = band
            table[2, e] = -band
            table[3, e] = jnp.full((SUB, LANES), 0.0 if grown is None else grown, f32)

    ids = [plane_of(group, q, group_planes) for q in range(QUAD)]

    def chunk(first, c, first_out):
        cells = [(u, q) for u in range(UNITS) for q in range(QUAD)]
        rows_of = [pl.ds(pl.multiple_of(first + SUB * u, SUB), SUB) for u in range(UNITS)]
        outs_of = [pl.ds(pl.multiple_of(first_out + SUB * u, SUB), SUB) for u in range(UNITS)]
        mean, after, f, held = {}, {}, {}, {}
        for u, q in cells:
            if moved:
                f[u, q] = refs[1][q, rows_of[u], c]
                held[u, q] = refs[1][QUAD + q, rows_of[u], c]
            else:
                f[u, q] = start_flux[ids[q], rows_of[u], c]
                held[u, q] = start_weight[ids[q], rows_of[u], c]
        for e in range(frames):
            value = [filtered[e][r, c] for r in rows_of]
            mask = [masks[night, e, r, c] for r in rows_of]
            gain, above, below, grown = (table[k, e] for k in range(4))
            for k in cells:
                u, q = k
                if e == lead:
                    after[k] = held[k] + table[3, frames - 1]
                    held[k] = jnp.maximum(held[k], weight_floor)
                    mean[k] = f[k] * pltpu.reciprocal(held[k], approx=True)
                if e < lead:
                    total = jnp.maximum(held[k], weight_floor)
                    mean[k] = f[k] * pltpu.reciprocal(total, approx=True)
                step = value[u] - mean[k]
                clipped = jnp.minimum(jnp.maximum(step, below), above)
                step = jnp.where((mask[u] & (1 << ids[q])) != 0, clipped, step)
                if e < lead:
                    f[k] = f[k] + gain * (mean[k] + step)
                    held[k] = held[k] + gain
                else:
                    part = gain * pltpu.reciprocal(held[k] + grown, approx=True)
                    mean[k] = mean[k] + part * step
        grown = table[3, frames - 1]
        for k in cells:
            u, q = k
            flux = mean[k] * (held[k] + grown)
            if last:
                out_flux[q // 2, 0, q % 2, outs_of[u], c] = flux
                out_weight[q // 2, 0, q % 2, outs_of[u], c] = after[k]
            else:
                out[q, outs_of[u], c] = flux
                out[QUAD + q, outs_of[u], c] = after[k]

    step_rows = SUB * UNITS

    def lanes(k):
        return pl.ds(pl.multiple_of(k * LANES, LANES), LANES)

    if last:
        i = pl.program_id(0)
        block = out_flux.shape[3]
        pl.when(i == 0)(prepare)

        @pl.loop(0, block // step_rows * tiles)
        def _(k):
            row = k // tiles * step_rows
            chunk(i * block + row, lanes(k % tiles), row)
    else:
        prepare()

        @pl.loop(0, rows // step_rows * tiles)
        def _(k):
            row = k // tiles * step_rows
            chunk(row, lanes(k % tiles), row)

        put_sides(info[0], out, DOWN, UP, 1, margin, (send_a, send_b))


def stack_night(info, offsets, weights, masks, images, state, night, planes, earlier, after):
    nights, frames, rows, cols = masks.shape
    margin = 3 * rows // 4
    side = 3 * cols // 4
    last = night == nights - 1
    scratch = [pltpu.VMEM((4, frames, SUB, LANES), f32)]
    if night > 0:
        scratch.append(pltpu.VMEM((FIELDS, rows, cols), f32))
        scratch += [pltpu.VMEM((rows, cols + side + LANES), f32)] * FIELDS
    args = (info, offsets, weights, masks, *images, *state)
    specs = [SMEM] * 3 + [VMEM] * (len(args) - 3)
    kernel = functools.partial(
        stack_kernel, night=night, last=last, margin=margin, side=side, planes=planes,
        parts=len(images), spare=len(earlier),
    )
    known = dict(
        scratch=scratch,
        flops=12 * frames * QUAD * rows * cols,
        name="stack_night",
        after=after,
    )
    if not last:
        strip = strip_shape(margin, cols)
        out = jax.ShapeDtypeStruct((FIELDS, rows, cols), f32)
        return call(kernel, (out, strip, strip), specs, args, **known)
    total, group = planes
    out = jax.ShapeDtypeStruct((2, total // QUAD, 2, rows, cols), f32)
    block = pl.BlockSpec((2, 1, 2, rows // BLOCKS, cols), lambda i: (0, group, 0, i, 0))
    return call(
        kernel,
        (out, out),
        specs + [pl.BlockSpec(memory_space=pl.ANY)] * len(earlier),
        (*args, *earlier),
        grid=(BLOCKS,),
        out_specs=(block, block),
        aliases={len(args) + i: i for i in range(len(earlier))},
        **known,
    )


def per_device(
    exposures, psf_kernels, clip_masks, exposure_weights, plane_offsets, start_flux, start_weight
):
    nights, frames, rows, cols = exposures.shape
    planes_total = start_flux.shape[0]
    radius = (psf_kernels.shape[2] - 1) // 2
    iy, ix = lax.axis_index("sy"), lax.axis_index("sx")
    ny, nx = lax.axis_size("sy"), lax.axis_size("sx")
    info = jnp.stack([iy % 2, ix % 2, iy, ix, jnp.int32(ny), jnp.int32(nx)]).astype(jnp.int32)

    offsets = jnp.swapaxes(plane_offsets, 1, 2)

    *sent, done = pack_cols(info, exposures, radius)
    got_cols = swap_columns(sent)
    bands, done = make_bands(psf_kernels, rows, (done,))
    *sent, done = pack_rows(info, exposures, got_cols, 0, 1, radius, (done,))
    rows_first = swap_rows(sent)
    *sent, done = pack_rows(info, exposures, got_cols, 1, nights - 1, radius, (done,))
    rows_later = swap_rows(sent)
    image, done = filter_night(
        info, exposures, 0, 0, bands, rows_first, got_cols, 0, frames, radius, (done,)
    )
    groups = [(planes_total, g) for g in range(planes_total // QUAD)]
    states = [(start_flux, start_weight)] * len(groups)
    results = ()
    for n in range(nights):
        fields = []
        sent = []
        for group, state in zip(groups, states):
            wait = tuple(rows_later) if n == 0 and group == groups[-1] else ()
            first, *strips, done = stack_night(
                info, offsets, exposure_weights, clip_masks, (image,), state, n, group, results,
                (done, *wait),
            )
            fields.append(first)
            if n == nights - 1:
                results = (first, *strips)
            else:
                sent.append(swap_rows(strips))
        if n == nights - 1:
            shape = (planes_total, rows, cols)
            return tuple(r.reshape(shape) for r in results)
        states = []
        for i, group in enumerate(groups):
            field, *strips, done = move_rows(
                info, offsets, fields[i], sent[i], n, group, (done,)
            )
            states.append((field, *swap_columns(strips)))
            if i == 0:
                image, done = filter_night(
                    info, exposures, n + 1, n, bands, rows_later, got_cols, 0, frames, radius,
                    (done,),
                )


def solution(mesh):
    return jax.shard_map(
        per_device,
        mesh=mesh,
        in_specs=(
            P(None, None, "sy", "sx"),
            P(),
            P(None, None, "sy", "sx"),
            P(),
            P(),
            P(None, "sy", "sx"),
            P(None, "sy", "sx"),
        ),
        out_specs=(P(None, "sy", "sx"), P(None, "sy", "sx")),
        check_vma=False,
    )
```

```python
import functools
import math

import jax
import jax.numpy as jnp
from jax import lax
from jax.experimental import pallas as pl
from jax.experimental.pallas import tpu as pltpu
from jax.sharding import PartitionSpec as P

band_scale = 1.5
weight_floor = 1.0
LANES = 128
SUB = 8
GROUP = 16
bf16 = jnp.bfloat16
f32 = jnp.float32
SMEM = pl.BlockSpec(memory_space=pltpu.SMEM)
VMEM = pl.BlockSpec(memory_space=pltpu.VMEM)


def call(
    kernel, outs, in_specs, args, *, name, flops, scratch=(), limit=16 << 20, after=(),
    grid=(), out_specs=None, aliases=None,
):
    size = sum(math.prod(o.shape) * o.dtype.itemsize for o in outs)
    known = len(args)
    begin = known + len(after)
    end = begin + len(outs)
    token = jax.ShapeDtypeStruct((SUB, LANES), f32)

    def ordered(*refs):
        refs[end][...] = jnp.zeros((SUB, LANES), f32)
        kernel(*refs[:known], *refs[begin:end], *refs[end + 1 :])

    return pl.pallas_call(
        ordered,
        grid=grid,
        out_shape=(*outs, token),
        in_specs=list(in_specs) + [VMEM] * len(after),
        out_specs=(VMEM,) * (len(outs) + 1) if out_specs is None else (*out_specs, VMEM),
        scratch_shapes=list(scratch),
        input_output_aliases=aliases or {},
        compiler_params=pltpu.CompilerParams(vmem_limit_bytes=limit),
        cost_estimate=pl.CostEstimate(flops=flops, bytes_accessed=2 * size, transcendentals=0),
        name=name,
    )(*args, *after)


def swap_pairs(axis, parity):
    ny, nx = lax.axis_size("sy"), lax.axis_size("sx")
    count, others = (ny, nx) if axis == "sy" else (nx, ny)
    pairs = []
    for j in range(others):
        for i in range(count):
            k = i + 1 if (i - parity) % 2 == 0 else i - 1
            if axis == "sx":
                k %= count
            target = (k, j) if 0 <= k < count else (i, j ^ 1)
            if axis == "sy":
                pairs.append((i * nx + j, target[0] * nx + target[1]))
            else:
                pairs.append((j * nx + i, target[1] * nx + target[0]))
    return pairs


def swap(value, axis, parity):
    return lax.ppermute(value, ("sy", "sx"), swap_pairs(axis, parity))


def swap_rows(values):
    return [swap(v, "sy", parity) for parity, v in enumerate(values)]


def swap_columns(values):
    return [swap(v, "sx", parity) for parity, v in enumerate(values)]


CODES = 32767.0
STEPS = 8.0


def put_codes(send, pieces):
    length, width = pieces[0]().shape
    row = lax.broadcasted_iota(jnp.int32, (GROUP, width), 0)
    scales = jnp.zeros((GROUP, width), f32)
    for j, piece in enumerate(pieces):
        v = piece()
        top = jnp.max(jnp.max(jnp.abs(v), axis=0, keepdims=True), axis=1, keepdims=True)
        power = jnp.ceil(jnp.log2(jnp.maximum(top, 1e-12)) * STEPS) + 1.0
        t = v * (jnp.exp2(power * (-1.0 / STEPS)) * (CODES * CODES))
        code = t * lax.rsqrt(jnp.abs(t) + 1e-30)
        send[length * j : length * (j + 1), :] = to_int16(code)
        scales = jnp.where(row == j, power, scales)
    send[length * len(pieces) :, :] = to_int16(scales)


def to_int16(v):
    return v.astype(jnp.int32).astype(jnp.int16)


def get_codes(use_first, first, second, count, keep):
    length = (first.shape[0] - GROUP) // count

    def rows(start, size):
        both = jnp.where(use_first, first[start : start + size, :], second[start : start + size, :])
        return both.astype(jnp.int32).astype(f32)

    scale = jnp.exp2(rows(length * count, GROUP) * (1.0 / STEPS)) * (keep / (CODES * CODES))

    def piece(j):
        code = rows(length * j, length)
        return code * (jnp.abs(code) + 1.0) * scale[j : j + 1, :]

    return piece


def lane_iota(shape):
    return lax.broadcasted_iota(jnp.int32, shape, len(shape) - 1)


def pack_cols_kernel(info, x, send_a, send_b, *, radius):
    nights, frames, rows, cols = x.shape
    even_x = info[1] == 0
    lane = lane_iota((rows, LANES))
    for n in range(nights):
        to_right = jnp.zeros((rows, LANES), bf16)
        to_left = jnp.zeros((rows, LANES), bf16)
        for e in range(frames):
            here = (lane >= radius * e) & (lane < radius * (e + 1))
            shift = (radius * (e + 1)) % LANES
            right = x[n, e, :, cols - LANES :]
            to_right = jnp.where(here, pltpu.roll(right, shift, 1), to_right)
            to_left = jnp.where(here, pltpu.roll(x[n, e, :, :LANES], radius * e, 1), to_left)
        send_a[n] = jnp.where(even_x, to_right, to_left)
        send_b[n] = jnp.where(even_x, to_left, to_right)


def pack_cols(info, exposures, radius):
    nights, frames, rows, cols = exposures.shape
    out = jax.ShapeDtypeStruct((nights, rows, LANES), bf16)
    return call(
        functools.partial(pack_cols_kernel, radius=radius),
        (out, out),
        [SMEM, VMEM],
        (info, exposures),
        flops=1 << 26,
        name="pack_cols",
    )


def received_cols(info, ca, cb, night):
    even_x = info[1] == 0
    zero = jnp.zeros((), bf16)
    left = jnp.where(info[3] > 0, jnp.where(even_x, cb[night], ca[night]), zero)
    right = jnp.where(info[3] < info[5] - 1, jnp.where(even_x, ca[night], cb[night]), zero)
    return left, right


def side_tile(left, right, e, radius):
    lane = lane_iota(left.shape)
    zero = jnp.zeros((), bf16)
    right = pltpu.roll(right, (LANES - radius * e) % LANES, 1)
    left = pltpu.roll(left, (2 * LANES - radius - radius * e) % LANES, 1)
    return jnp.where(lane < radius, right, jnp.where(lane >= LANES - radius, left, zero))


def pack_rows_kernel(info, x, ca, cb, send_a, send_b, *, radius, first):
    frames, tile_rows, cols = x.shape[1:]
    rows = frames * radius
    even = info[0] == 0
    shape = (rows, frames * GROUP)
    r = lax.broadcasted_iota(jnp.int32, shape, 0)
    c = lax.broadcasted_iota(jnp.int32, shape, 1)
    base = (r // radius) * GROUP + r % radius
    sel_top = (c == base).astype(bf16)
    sel_bot = (c == base + (GROUP - radius)).astype(bf16)
    for n in range(send_a.shape[0]):
        left, right = received_cols(info, ca, cb, first + n)

        def strip(sel, start):
            at = slice(start, start + GROUP)
            ends = [side_tile(left[at], right[at], e, radius) for e in range(frames)]
            block = x[first + n, :, at, :].reshape(frames * GROUP, cols)
            block = jnp.concatenate([block, jnp.concatenate(ends, axis=0)], axis=1)
            return jnp.dot(sel, block, preferred_element_type=f32).astype(bf16)

        up = strip(sel_top, 0)
        down = strip(sel_bot, tile_rows - GROUP)
        send_a[n] = jnp.where(even, down, up)
        send_b[n] = jnp.where(even, up, down)


def pack_rows(info, exposures, got_cols, first, count, radius, after):
    nights, frames, rows, cols = exposures.shape
    out = jax.ShapeDtypeStruct((count, frames * radius, cols + LANES), bf16)
    return call(
        functools.partial(pack_rows_kernel, radius=radius, first=first),
        (out, out),
        [SMEM] + [VMEM] * 3,
        (info, exposures, *got_cols),
        flops=1 << 26,
        name="pack_rows",
        after=after,
    )


STRIDE = 3


def band_shape(rows, size):
    pitch = rows + 2 * GROUP
    count = -(-size // STRIDE)
    ring = -(-(pitch * count + 2 * GROUP) // LANES) * LANES
    return pitch, count, ring


def bands_kernel(psf, out, *, rows):
    _, size, frames, _ = psf.shape
    nights = out.shape[0]
    radius = (size - 1) // 2
    pitch, count, ring = band_shape(rows, size)
    shape = (size, STRIDE * ring)
    b = lax.broadcasted_iota(jnp.int32, shape, 0)
    c = lax.broadcasted_iota(jnp.int32, shape, 1)
    key = c - (b % STRIDE) * ring - pitch * (b // STRIDE) + radius
    key = jnp.where(key >= ring, key - ring, key)
    key = jnp.where(c // ring == b % STRIDE, key, -1)
    total = jnp.zeros((nights * frames, STRIDE * ring), f32)
    for a in range(size):
        taps = jnp.concatenate([psf[n, a] for n in range(nights)], axis=0)
        total = total + jnp.dot(taps, (key == a).astype(bf16), preferred_element_type=f32)
    for e in range(nights * frames):
        for g in range(STRIDE):
            row = total[e : e + 1, ring * g : ring * (g + 1)]
            row = jnp.broadcast_to(row, (rows, ring))
            band = pltpu.roll(row, 0, 1, stride=1, stride_axis=0).astype(bf16)
            out[e // frames, e % frames, rows * g : rows * (g + 1), :] = band


def make_bands(psf_kernels, rows, after):
    nights, frames, size, _ = psf_kernels.shape
    ring = band_shape(rows, size)[2]
    return call(
        functools.partial(bands_kernel, rows=rows),
        (jax.ShapeDtypeStruct((nights, frames, STRIDE * rows, ring), bf16),),
        [VMEM],
        (jnp.swapaxes(psf_kernels, 1, 2),),
        flops=1 << 28,
        name="make_bands",
        limit=24 << 20,
        after=after,
    )


def filter_kernel(
    info, x, ra, rb, ca, cb, bands, out, border, image_0, image_1, windows_0, windows_1,
    *, radius, night, half, start
):
    frames, rows, cols = out.shape
    tiles = cols // LANES
    size = 2 * radius + 1
    pitch, count, ring = band_shape(rows, size)
    packed = ra.shape[1]
    extra = pitch - rows
    even_y = info[0] == 0
    zero = jnp.zeros((), bf16)
    top_ok = info[2] > 0
    bot_ok = info[2] < info[4] - 1
    col_l, col_r = received_cols(info, ca, cb, night)
    top = jnp.where(even_y, rb[half], ra[half])
    bot = jnp.where(even_y, ra[half], rb[half])
    top = jnp.where(top_ok, top, zero)
    bot = jnp.where(bot_ok, bot, zero)
    top = pltpu.roll(top, cols + LANES - STRIDE, 1)
    shape = (frames * extra, packed)
    r = lax.broadcasted_iota(jnp.int32, shape, 0)
    c = lax.broadcasted_iota(jnp.int32, shape, 1)
    frame, place = r // extra + start, r % extra
    sel_bot = ((place < radius) & (c == frame * radius + place)).astype(bf16)
    from_top = place - (extra - radius)
    sel_top = ((from_top >= 0) & (c == frame * radius + from_top)).astype(bf16)
    border[...] = (
        jnp.dot(sel_bot, bot, preferred_element_type=f32)
        + jnp.dot(sel_top, top, preferred_element_type=f32)
    ).astype(bf16)

    lane = lane_iota((rows, LANES))
    lane_all = lane_iota((pitch, LANES))
    first = pitch * count
    last = ring - extra
    if last > first:
        for windows in (windows_0, windows_1):
            windows[first:last, :] = jnp.zeros((last - first, cols + LANES), bf16)

    def turn(shift, source, mask_lane):
        if shift == 0:
            return source
        turned = [pltpu.roll(t, shift % LANES, 1) for t in source]
        size = len(source)
        if shift > 0:
            return [jnp.where(mask_lane < shift, turned[k - 1], turned[k]) for k in range(size)]
        return [
            jnp.where(mask_lane < LANES + shift, turned[k], turned[(k + 1) % size])
            for k in range(size)
        ]

    middle = (STRIDE - 1) // 2

    def prepare(e, image, windows):
        image[:rows, :cols] = x[night, start + e]
        image[:rows, cols:] = side_tile(col_l, col_r, start + e, radius)
        image[rows:] = border[e * extra : (e + 1) * extra]
        parts = [image[:, LANES * k : LANES * (k + 1)] for k in range(tiles + 1)]
        for w in range(count):
            shift = radius - middle - STRIDE * w
            for k, value in enumerate(turn(shift, parts, lane_all)):
                windows[pitch * w : pitch * (w + 1), LANES * k : LANES * (k + 1)] = value
        tail = [t[rows:] for t in parts]
        for k, value in enumerate(turn(radius - middle + STRIDE, tail, lane_all[:extra])):
            windows[last:, LANES * k : LANES * (k + 1)] = value

    def combine(e, windows):
        sums = jnp.dot(bands[night, start + e], windows[...], preferred_element_type=f32)
        total = None
        for g in range(STRIDE):
            part = sums[rows * g : rows * (g + 1)]
            part = [part[:, LANES * k : LANES * (k + 1)] for k in range(tiles + 1)]
            part = turn(middle - g, part, lane)
            total = part if total is None else [a + b for a, b in zip(total, part)]
        for k in range(tiles):
            out[e, :, LANES * k : LANES * (k + 1)] = total[k]

    buffers = ((image_0, windows_0), (image_1, windows_1))
    prepare(0, *buffers[0])
    for e in range(frames):
        if e + 1 < frames:
            prepare(e + 1, *buffers[(e + 1) % 2])
        combine(e, buffers[e % 2][1])


def filter_night(
    info, exposures, night, half, bands, got_rows, got_cols, start, count, radius, after
):
    nights, frames, rows, cols = exposures.shape
    pitch, _, ring = band_shape(rows, 2 * radius + 1)
    return call(
        functools.partial(filter_kernel, radius=radius, night=night, half=half, start=start),
        (jax.ShapeDtypeStruct((count, rows, cols), f32),),
        [SMEM] + [VMEM] * 6,
        (info, exposures, *got_rows, *got_cols, bands),
        scratch=[
            pltpu.VMEM((count * 2 * GROUP, cols + LANES), bf16),
            pltpu.VMEM((pitch, cols + LANES), bf16),
            pltpu.VMEM((pitch, cols + LANES), bf16),
            pltpu.VMEM((ring, cols + LANES), bf16),
            pltpu.VMEM((ring, cols + LANES), bf16),
        ],
        after=after,
        flops=2 * count * STRIDE * rows * ring * cols,
        name="filter_night",
    )


QUAD = 4
UNITS = 4
BLOCKS = 2
FIELDS = 2 * QUAD
DOWN, UP = (0, 1, 4, 5), (2, 3, 6, 7)
RIGHT, LEFT = (0, 2, 4, 6), (1, 3, 5, 7)


def plane_of(group, q, planes):
    return (q // 2) * (planes // 2) + 2 * group + q % 2


def strip_shape(length, width):
    return jax.ShapeDtypeStruct((len(DOWN) * length + GROUP, width), jnp.int16)


def put_sides(odd, source, first_way, second_way, axis, margin, sends):
    size = source.shape[axis]
    end = pl.multiple_of((size - margin) * (1 - odd), SUB if axis == 1 else LANES)
    begin = pl.multiple_of((size - margin) * odd, SUB if axis == 1 else LANES)
    for send, start, swapped in ((sends[0], end, odd), (sends[1], begin, 1 - odd)):
        cut = pl.ds(start, margin)

        def piece(a, b, cut=cut, swapped=swapped):
            f = a + (b - a) * swapped
            return lambda: source[f, cut, :] if axis == 1 else source[f, :, cut]

        put_codes(send, [piece(a, b) for a, b in zip(first_way, second_way)])


def move_rows_kernel(
    info, offsets, field, ra, rb, out, send_a, send_b, *above, margin, side, night, planes
):
    group_planes, group = planes
    fields, rows, cols = field.shape
    even = info[0] == 0
    top_ok = jnp.where(info[2] > 0, 1.0, 0.0)
    bot_ok = jnp.where(info[2] < info[4] - 1, 1.0, 0.0)
    sub = lax.broadcasted_iota(jnp.int32, (SUB, LANES), 0)

    def turn(source, start, result):
        base = (start // SUB) * SUB
        rest = start % SUB
        back = (SUB - rest) % SUB
        keep = sub < SUB - rest
        for k in range(cols // LANES):
            lanes = slice(LANES * k, LANES * (k + 1))
            turned = None
            for j in range(rows // SUB + 1):
                before = turned
                at = pl.ds(pl.multiple_of(base + SUB * j, SUB), SUB)
                turned = pltpu.roll(source[at, lanes], back, 0)
                if j:
                    result[SUB * (j - 1) : SUB * j, lanes] = jnp.where(keep, before, turned)

    from_above = get_codes(even, rb, ra, len(DOWN), top_ok)
    from_below = get_codes(even, ra, rb, len(UP), bot_ok)
    for j in range(len(DOWN)):
        for f, got in ((DOWN[j], from_above), (UP[j], from_below)):
            source = above[f]
            offset = offsets[night, 0, plane_of(group, f % QUAD, group_planes)]
            if f in DOWN:
                source[:margin] = got(j)
                source[margin : margin + rows] = field[f]
                start = margin - offset
            else:
                source[:rows] = field[f]
                source[rows : rows + margin] = got(j)
                start = -offset
            source[rows + margin :] = jnp.zeros((SUB, cols), f32)
            turn(source, start, out.at[f])
    put_sides(info[1], out, RIGHT, LEFT, 2, side, (send_a, send_b))


def move_rows(info, offsets, field, recv, night, planes, after):
    fields, rows, cols = field.shape
    margin = 3 * rows // 4
    side = 3 * cols // 4
    strip = strip_shape(rows, side)
    return call(
        functools.partial(
            move_rows_kernel, margin=margin, side=side, night=night, planes=planes
        ),
        (jax.ShapeDtypeStruct(field.shape, f32), strip, strip),
        [SMEM, SMEM, VMEM, VMEM, VMEM],
        (info, offsets, field, *recv),
        scratch=[pltpu.VMEM((rows + margin + SUB, cols), f32)] * fields,
        flops=1 << 27,
        after=after,
        name="move_rows",
    )


def move_columns(info, offsets, night, field, ca, cb, out, wide, side, planes):
    group_planes, group = planes
    fields, rows, cols = field.shape
    even = info[1] == 0
    left_ok = jnp.where(info[3] > 0, 1.0, 0.0)
    right_ok = jnp.where(info[3] < info[5] - 1, 1.0, 0.0)
    lane = lane_iota((SUB, LANES))

    def turn(source, start, result):
        base = (start // LANES) * LANES
        rest = start % LANES
        back = (LANES - rest) % LANES
        keep = lane < LANES - rest
        for k in range(rows // SUB):
            at = slice(SUB * k, SUB * (k + 1))
            turned = None
            for j in range(cols // LANES + 1):
                before = turned
                lanes = pl.ds(pl.multiple_of(base + LANES * j, LANES), LANES)
                turned = pltpu.roll(source[at, lanes], back, 1)
                if j:
                    result[at, LANES * (j - 1) : LANES * j] = jnp.where(keep, before, turned)

    from_left = get_codes(even, cb, ca, len(RIGHT), left_ok)
    from_right = get_codes(even, ca, cb, len(LEFT), right_ok)
    for j in range(len(RIGHT)):
        for f, got in ((RIGHT[j], from_left), (LEFT[j], from_right)):
            source = wide[f]
            offset = offsets[night, 1, plane_of(group, f % QUAD, group_planes)]
            if f in RIGHT:
                source[:, :side] = got(j)
                source[:, side : side + cols] = field[f]
                start = side - offset
            else:
                source[:, :cols] = field[f]
                source[:, cols : cols + side] = got(j)
                start = -offset
            source[:, cols + side :] = jnp.zeros((rows, LANES), f32)
            turn(source, start, out.at[f])


def stack_kernel(*refs, night, last, margin, side, planes, parts, spare):
    info, offsets, weights, masks, *refs = refs
    images, refs = refs[:parts], refs[parts:]
    filtered = [part.at[e] for part in images for e in range(part.shape[0])]
    moved = night > 0
    group_planes, group = planes
    if moved:
        field, ca, cb, *refs = refs
        _, rows, cols = field.shape
    else:
        start_flux, start_weight, *refs = refs
        rows, cols = start_flux.shape[1:]
    refs = refs[spare:]
    if last:
        out_flux, out_weight, *refs = refs
    else:
        out, send_a, send_b, *refs = refs
    table = refs[0]
    frames = len(filtered)
    tiles = cols // LANES
    lead = 2 if moved else 0

    def prepare():
        if moved:
            move_columns(
                info, offsets, night - 1, field, ca, cb, refs[1], refs[2:], side, planes
            )
        grown = None
        for e in range(frames):
            gain = weights[night, e]
            if e >= lead:
                grown = gain if grown is None else grown + gain
            filled = jnp.full((SUB, LANES), gain, f32)
            band = band_scale / jnp.sqrt(filled)
            table[0, e] = filled
            table[1, e] = band
            table[2, e] = -band
            table[3, e] = jnp.full((SUB, LANES), 0.0 if grown is None else grown, f32)

    ids = [plane_of(group, q, group_planes) for q in range(QUAD)]

    def chunk(first, c, first_out):
        cells = [(u, q) for u in range(UNITS) for q in range(QUAD)]
        rows_of = [pl.ds(pl.multiple_of(first + SUB * u, SUB), SUB) for u in range(UNITS)]
        outs_of = [pl.ds(pl.multiple_of(first_out + SUB * u, SUB), SUB) for u in range(UNITS)]
        mean, after, f, held = {}, {}, {}, {}
        for u, q in cells:
            if moved:
                f[u, q] = refs[1][q, rows_of[u], c]
                held[u, q] = refs[1][QUAD + q, rows_of[u], c]
            else:
                f[u, q] = start_flux[ids[q], rows_of[u], c]
                held[u, q] = start_weight[ids[q], rows_of[u], c]
        for e in range(frames):
            value = [filtered[e][r, c] for r in rows_of]
            mask = [masks[night, e, r, c] for r in rows_of]
            gain, above, below, grown = (table[k, e] for k in range(4))
            for k in cells:
                u, q = k
                if e == lead:
                    after[k] = held[k] + table[3, frames - 1]
                    held[k] = jnp.maximum(held[k], weight_floor)
                    mean[k] = f[k] * pltpu.reciprocal(held[k], approx=True)
                if e < lead:
                    total = jnp.maximum(held[k], weight_floor)
                    mean[k] = f[k] * pltpu.reciprocal(total, approx=True)
                step = value[u] - mean[k]
                clipped = jnp.minimum(jnp.maximum(step, below), above)
                step = jnp.where((mask[u] & (1 << ids[q])) != 0, clipped, step)
                if e < lead:
                    f[k] = f[k] + gain * (mean[k] + step)
                    held[k] = held[k] + gain
                else:
                    part = gain * pltpu.reciprocal(held[k] + grown, approx=True)
                    mean[k] = mean[k] + part * step
        grown = table[3, frames - 1]
        for k in cells:
            u, q = k
            flux = mean[k] * (held[k] + grown)
            if last:
                out_flux[q // 2, 0, q % 2, outs_of[u], c] = flux
                out_weight[q // 2, 0, q % 2, outs_of[u], c] = after[k]
            else:
                out[q, outs_of[u], c] = flux
                out[QUAD + q, outs_of[u], c] = after[k]

    step_rows = SUB * UNITS

    def lanes(k):
        return pl.ds(pl.multiple_of(k * LANES, LANES), LANES)

    if last:
        i = pl.program_id(0)
        block = out_flux.shape[3]
        pl.when(i == 0)(prepare)

        @pl.loop(0, block // step_rows * tiles)
        def _(k):
            row = k // tiles * step_rows
            chunk(i * block + row, lanes(k % tiles), row)
    else:
        prepare()

        @pl.loop(0, rows // step_rows * tiles)
        def _(k):
            row = k // tiles * step_rows
            chunk(row, lanes(k % tiles), row)

        put_sides(info[0], out, DOWN, UP, 1, margin, (send_a, send_b))


def stack_night(info, offsets, weights, masks, images, state, night, planes, earlier, after):
    nights, frames, rows, cols = masks.shape
    margin = 3 * rows // 4
    side = 3 * cols // 4
    last = night == nights - 1
    scratch = [pltpu.VMEM((4, frames, SUB, LANES), f32)]
    if night > 0:
        scratch.append(pltpu.VMEM((FIELDS, rows, cols), f32))
        scratch += [pltpu.VMEM((rows, cols + side + LANES), f32)] * FIELDS
    args = (info, offsets, weights, masks, *images, *state)
    specs = [SMEM] * 3 + [VMEM] * (len(args) - 3)
    kernel = functools.partial(
        stack_kernel, night=night, last=last, margin=margin, side=side, planes=planes,
        parts=len(images), spare=len(earlier),
    )
    known = dict(
        scratch=scratch,
        flops=12 * frames * QUAD * rows * cols,
        name="stack_night",
        after=after,
    )
    if not last:
        strip = strip_shape(margin, cols)
        out = jax.ShapeDtypeStruct((FIELDS, rows, cols), f32)
        return call(kernel, (out, strip, strip), specs, args, **known)
    total, group = planes
    out = jax.ShapeDtypeStruct((2, total // QUAD, 2, rows, cols), f32)
    block = pl.BlockSpec((2, 1, 2, rows // BLOCKS, cols), lambda i: (0, group, 0, i, 0))
    return call(
        kernel,
        (out, out),
        specs + [pl.BlockSpec(memory_space=pl.ANY)] * len(earlier),
        (*args, *earlier),
        grid=(BLOCKS,),
        out_specs=(block, block),
        aliases={len(args) + i: i for i in range(len(earlier))},
        **known,
    )


def per_device(
    exposures, psf_kernels, clip_masks, exposure_weights, plane_offsets, start_flux, start_weight
):
    nights, frames, rows, cols = exposures.shape
    planes_total = start_flux.shape[0]
    radius = (psf_kernels.shape[2] - 1) // 2
    iy, ix = lax.axis_index("sy"), lax.axis_index("sx")
    ny, nx = lax.axis_size("sy"), lax.axis_size("sx")
    info = jnp.stack([iy % 2, ix % 2, iy, ix, jnp.int32(ny), jnp.int32(nx)]).astype(jnp.int32)

    offsets = jnp.swapaxes(plane_offsets, 1, 2)

    *sent, done = pack_cols(info, exposures, radius)
    got_cols = swap_columns(sent)
    bands, done = make_bands(psf_kernels, rows, (done,))
    *sent, done = pack_rows(info, exposures, got_cols, 0, 1, radius, (done,))
    rows_first = swap_rows(sent)
    *sent, done = pack_rows(info, exposures, got_cols, 1, nights - 1, radius, (done,))
    rows_later = swap_rows(sent)
    image, done = filter_night(
        info, exposures, 0, 0, bands, rows_first, got_cols, 0, frames, radius, (done,)
    )
    groups = [(planes_total, g) for g in range(planes_total // QUAD)]
    states = [(start_flux, start_weight)] * len(groups)
    results = ()
    for n in range(nights):
        fields = []
        sent = []
        for group, state in zip(groups, states):
            wait = tuple(rows_later) if n == 0 and group == groups[-1] else ()
            first, *strips, done = stack_night(
                info, offsets, exposure_weights, clip_masks, (image,), state, n, group, results,
                (done, *wait),
            )
            fields.append(first)
            if n == nights - 1:
                results = (first, *strips)
            else:
                sent.append(swap_rows(strips))
        if n == nights - 1:
            shape = (planes_total, rows, cols)
            return tuple(r.reshape(shape) for r in results)
        states = []
        for i, group in enumerate(groups):
            field, *strips, done = move_rows(
                info, offsets, fields[i], sent[i], n, group, (done,)
            )
            states.append((field, *swap_columns(strips)))
            if i == 0:
                image, done = filter_night(
                    info, exposures, n + 1, n, bands, rows_later, got_cols, 0, frames, radius,
                    (done,),
                )


def solution(mesh):
    return jax.shard_map(
        per_device,
        mesh=mesh,
        in_specs=(
            P(None, None, "sy", "sx"),
            P(),
            P(None, None, "sy", "sx"),
            P(),
            P(),
            P(None, "sy", "sx"),
            P(None, "sy", "sx"),
        ),
        out_specs=(P(None, "sy", "sx"), P(None, "sy", "sx")),
        check_vma=False,
    )
```
